32 devices in a mesh: gx: 8 (over y, x, core), gy: 4 (over z).
Axes of the slice: x: 2, y: 2, z: 4, core: 2. Of those that a mesh axis runs over, the one named last changes fastest.
Arguments:
- rhs_field: float32 [64, 128, 256], P('gx', 'gy'), may hold values from -50 to 50
- alpha_coef: float32 [64, 128, 256], P('gx', 'gy'), may hold values from 0.2 to 5
- beta_coef: float32 [64, 128, 256], P('gx', 'gy'), may hold values from 0.3 to 27
Outputs:
- solution: float32 [64, 128, 256], P('gx', 'gy')
The draws below stay inside these ranges and needn't reach their ends.
All inputs are finite; a program needn't handle non-finite values.
Results may differ from the reference program's by a relative error of at most 0.0001.
Values sent between devices are 32-bit elements; how exact they have to be, the bound alone decides.
A program may use at most 128 MiB of HBM per device.

```python
import math
import jax
import jax.numpy as jnp

LEVELS = 4
PRE_STEPS = 3
POST_STEPS = 3
COARSE_STEPS = 8
NX = 64
NY = 128
NZ = 256


def draw_rhs_field(key, part):
    noise = 10.0 * jax.random.normal(key, (NX, NY, NZ), jnp.float32)
    return jnp.clip(noise, -50.0, 50.0)


def draw_beta_coef(key, part):
    unit = jax.random.uniform(key, (NX, NY, NZ), jnp.float32)
    base = 0.3 * jnp.exp(unit * math.log(10.0))
    xpos = jnp.arange(NX, dtype=jnp.float32) / max(NX - 1, 1)
    ramp = 1.0 + 2.0 * xpos
    return base * ramp[:, None, None]


def level_of(key, extent, cuts, low, largest):
    loudness, own = 1.0, jax.random.fold_in(key, 6)
    for axis_at, shards_of in cuts:
        heights = jnp.exp(jax.random.uniform(jax.random.fold_in(own, axis_at), (shards_of,), jnp.float32, low / len(cuts), largest / len(cuts)))
        loudness = loudness * jnp.repeat(heights, extent[axis_at] // shards_of).reshape([-1 if axis == axis_at else 1 for axis in range(len(extent))])
    return loudness


def setup_inputs(seed: int = 0) -> dict:
    streams_of = jax.random.split(jax.random.key(seed), 4)
    rhs_field = draw_rhs_field(jax.random.fold_in(streams_of[3], 71), 0)
    alpha_coef = jnp.clip(jnp.exp(math.log(5.0) - 3.218876 * jax.random.uniform(streams_of[1], (NX, NY, NZ), jnp.float32) ** level_of(streams_of[1], (NX, NY, NZ), ((0, 8), (1, 4)), -0.2, 0.2)), 0.2, 5.0)
    beta_coef = draw_beta_coef(jax.random.fold_in(streams_of[3], 71), 0)
    return dict(rhs_field=rhs_field, alpha_coef=alpha_coef, beta_coef=beta_coef)


HELM_SHIFT = 0.05
LOW_FRACTION = 0.1


def restrict(values):
    first, second, third = values.shape
    return values.reshape(first // 2, 2, second // 2, 2, third // 2, 2).mean(axis=(1, 3, 5))


def prolong(values):
    return jnp.repeat(jnp.repeat(jnp.repeat(values, 2, 0), 2, 1), 2, 2)


def zero_pad(values):
    return jnp.pad(values, 1)


def neighbours(padded):
    return [padded[2:, 1:-1, 1:-1], padded[:-2, 1:-1, 1:-1], padded[1:-1, 2:, 1:-1],
            padded[1:-1, :-2, 1:-1], padded[1:-1, 1:-1, 2:], padded[1:-1, 1:-1, :-2]]


def apply_op(u_padded, b_padded, alpha_level, inv_spacing):
    field = u_padded[1:-1, 1:-1, 1:-1]
    interior = b_padded[1:-1, 1:-1, 1:-1]
    summed = jnp.zeros_like(field)
    for near_u, near_b in zip(neighbours(u_padded), neighbours(b_padded)):
        summed = summed + (interior + near_b) * (field - near_u)
    return HELM_SHIFT * alpha_level * field + (0.5 * inv_spacing) * summed


def smooth(field, source, alpha_level, b_padded, inv_spacing, upper, sweeps, start_zero, padder):
    lower = LOW_FRACTION * upper
    middle = 0.5 * (upper + lower)
    half_width = 0.5 * (upper - lower)
    scaled = middle / half_width
    factor = 1.0 / scaled
    if start_zero:
        residual = source
    else:
        residual = source - apply_op(padder(field), b_padded, alpha_level, inv_spacing)
    direction = residual / middle
    field = direction if start_zero else field + direction
    for k in range(1, sweeps):
        residual = source - apply_op(padder(field), b_padded, alpha_level, inv_spacing)
        factor_new = 1.0 / (2.0 * scaled - factor)
        direction = factor_new * factor * direction + (2.0 * factor_new / half_width) * residual
        field = field + direction
        factor = factor_new
    return field


def reference(rhs_field, alpha_coef, beta_coef):
    alphas = [alpha_coef]
    betas = [beta_coef]
    for level_idx in range(1, LEVELS):
        alphas.append(restrict(alphas[-1]))
        betas.append(restrict(betas[-1]))
    uppers = [HELM_SHIFT * jnp.max(alphas[i]) + 12.0 * jnp.max(betas[i]) / 4.0 ** i for i in range(LEVELS)]
    b_pads = [zero_pad(b) for b in betas]
    sources = [rhs_field]
    fields = []
    for level_idx in range(LEVELS - 1):
        inv_spacing = 1.0 / 4.0 ** level_idx
        smoothed = smooth(jnp.zeros_like(sources[level_idx]), sources[level_idx], alphas[level_idx],
                          b_pads[level_idx], inv_spacing, uppers[level_idx], PRE_STEPS, True, zero_pad)
        residual = sources[level_idx] - apply_op(zero_pad(smoothed), b_pads[level_idx], alphas[level_idx], inv_spacing)
        sources.append(restrict(residual))
        fields.append(smoothed)
    last = LEVELS - 1
    coarse = smooth(jnp.zeros_like(sources[last]), sources[last], alphas[last], b_pads[last],
                    1.0 / 4.0 ** last, uppers[last], COARSE_STEPS, True, zero_pad)
    for level_idx in range(LEVELS - 2, -1, -1):
        smoothed = fields[level_idx] + prolong(coarse)
        coarse = smooth(smoothed, sources[level_idx], alphas[level_idx], b_pads[level_idx],
                        1.0 / 4.0 ** level_idx, uppers[level_idx], POST_STEPS, False, zero_pad)
    return coarse
```

```python
import functools

import jax
import jax.numpy as jnp
from jax import lax
from jax.experimental import pallas as pl
from jax.experimental.pallas import tpu as pltpu
from jax.sharding import PartitionSpec as P

PRE_STEPS = 3
POST_STEPS = 3
COARSE_STEPS = 8
HELM_SHIFT = 0.05
LOW_FRACTION = 0.1
LANES = 128
HALO = 3
MESH = pl.DeviceIdType.MESH
DIRS = [(1, 0), (-1, 0), (0, 1), (0, -1), (1, 1), (1, -1), (-1, 1), (-1, -1)]
HIGH = lax.Precision.HIGHEST


def dot(a, b):
    return jnp.dot(a, b, precision=HIGH, preferred_element_type=jnp.float32)


def iota(shape, dim):
    return lax.broadcasted_iota(jnp.int32, shape, dim)


def pick(rows, cols, cond):
    return cond(iota((rows, cols), 0), iota((rows, cols), 1)).astype(jnp.float32)


def roll(x, shift, axis):
    return pltpu.roll(x, shift % x.shape[axis], axis)


def restrict_sum(values, out_lanes):
    planes, rows, lanes = values.shape
    pairs = values.reshape(planes // 2, 2, rows, lanes)
    summed = (pairs[:, 0] + pairs[:, 1]).reshape(planes // 2 * rows, lanes)
    narrow = dot(summed, pick(lanes, out_lanes, lambda i, j: (i >> 1) == j))
    total = planes // 2 * rows
    small = dot(pick(total // 2, total, lambda i, j: (j >> 1) == i), narrow)
    return (0.125 * small).reshape(planes // 2, rows // 2, out_lanes)


class Exchange:
    def __init__(self, buf, st_next, st_prev, sems, slot, x_len, y_len, place, peers):
        self.buf, self.st_next, self.st_prev = buf, st_next, st_prev
        self.send, self.recv = sems
        self.slot, self.x_len, self.y_len = slot, x_len, y_len
        self.place, self.peers = place, peers

    def region(self, dx, dy):
        x_len, y_len = self.x_len, self.y_len
        if dx == 0:
            src_x = dst_x = pl.ds(HALO, x_len)
        elif dx == 1:
            src_x, dst_x = pl.ds(x_len, HALO), pl.ds(0, HALO)
        else:
            src_x, dst_x = pl.ds(HALO, HALO), pl.ds(x_len + HALO, HALO)
        if dy == 0:
            return (self.buf.at[:, src_x, pl.ds(0, y_len)],
                    self.buf.at[:, dst_x, pl.ds(0, y_len)])
        if dy == 1:
            return self.buf.at[:, src_x, pl.ds(y_len - 8, 8)], self.st_prev.at[:, dst_x]
        return self.buf.at[:, src_x, pl.ds(0, 8)], self.st_next.at[:, dst_x]

    def inside(self, dx, dy):
        x, y = self.place[0] + dx, self.place[1] + dy
        return (x >= 0) & (x < self.peers[0]) & (y >= 0) & (y < self.peers[1])

    def copy(self, k):
        dx, dy = DIRS[k]
        src, dst = self.region(dx, dy)
        return pltpu.make_async_remote_copy(
            src_ref=src, dst_ref=dst,
            send_sem=self.send.at[self.slot, k], recv_sem=self.recv.at[self.slot, k],
            device_id=(self.place[0] + dx, self.place[1] + dy), device_id_type=MESH)

    def clear(self):
        for dx, dy in DIRS:
            @pl.when(jnp.logical_not(self.inside(-dx, -dy)))
            def _():
                _, dst = self.region(dx, dy)
                dst[...] = jnp.zeros(dst.shape, jnp.float32)

    def start(self):
        for k, (dx, dy) in enumerate(DIRS):
            @pl.when(self.inside(dx, dy))
            def _():
                self.copy(k).start()

    def finish(self):
        for k, (dx, dy) in enumerate(DIRS):
            @pl.when(self.inside(dx, dy))
            def _():
                self.copy(k).wait_send()

            @pl.when(self.inside(-dx, -dy))
            def _():
                self.copy(k).wait_recv()
        shape = self.st_next.shape
        near = iota(shape, 2) < 4
        self.buf[:, :, pl.ds(self.y_len, 8)] = jnp.where(near, self.st_next[...], self.st_prev[...])


def over(start, count, chunk, body):
    if count == chunk:
        body(start)
        return

    def step(i, carry):
        body(start + i * chunk)
        return carry

    lax.fori_loop(0, count // chunk, step, 0)


def build(level, start, count, chunk, alpha_at, beta_at, z_len, wrap_y, coefs):
    dia, c_x, c_y, c_z = coefs
    h = 0.5 / 4.0**level

    def body(i):
        b = beta_at(i)
        up, down = beta_at(i + 1), beta_at(i - 1)
        shape = b.shape
        lane, row = iota(shape, 2), iota(shape, 1)
        y_up, y_down = roll(b, -1, 1), roll(b, 1, 1)
        if not wrap_y:
            y_up = jnp.where(row == shape[1] - 1, 0.0, y_up)
            y_down = jnp.where(row == 0, 0.0, y_down)
        z_up = jnp.where(lane == z_len - 1, 0.0, roll(b, -1, 2))
        z_down = jnp.where(lane == 0, 0.0, roll(b, 1, 2))
        total = 6.0 * b + (up + down) + (y_up + y_down) + (z_up + z_down)
        dia[pl.ds(i, chunk)] = HELM_SHIFT * alpha_at(i) + h * total
        for out, near in ((c_x, up), (c_y, y_up), (c_z, z_up)):
            out[pl.ds(i, chunk)] = jnp.where(jnp.minimum(b, near) > 0.0, h * (b + near), 0.0)

    over(start, count, chunk, body)


def apply_op(coefs, u, i, chunk):
    dia, c_x, c_y, c_z = coefs
    here = pl.ds(i, chunk)
    mid = u[here]
    y_c, z_c = c_y[here], c_z[here]
    off = c_x[here] * u[pl.ds(i + 1, chunk)] + c_x[pl.ds(i - 1, chunk)] * u[pl.ds(i - 1, chunk)]
    off += y_c * roll(mid, -1, 1) + roll(y_c * mid, 1, 1)
    off += z_c * roll(mid, -1, 2) + roll(z_c * mid, 1, 2)
    return mid, dia[here] * mid - off


def cheb(upper, steps):
    lower = LOW_FRACTION * upper
    middle, half = 0.5 * (upper + lower), 0.5 * (upper - lower)
    scaled = middle / half
    factor = 1.0 / scaled
    out = [(None, 1.0 / middle)]
    for _ in range(1, steps):
        new = 1.0 / (2.0 * scaled - factor)
        out.append((new * factor, 2.0 * new / half))
        factor = new
    return out


def sweep(coefs, u, u_new, d, f_at, a, b, start, count, chunk):
    def body(i):
        mid, au = apply_op(coefs, u, i, chunk)
        step = b * (f_at(i) - au)
        if a is not None:
            step += a * d[pl.ds(i, chunk)]
        d[pl.ds(i, chunk)] = step
        u_new[pl.ds(i, chunk)] = mid + step

    over(start, count, chunk, body)


def first(u, d, f_at, b, start, count, chunk):
    def body(i):
        step = b * f_at(i)
        d[pl.ds(i, chunk)] = step
        u[pl.ds(i, chunk)] = step

    over(start, count, chunk, body)


def residual(coefs, u, f_at, res, start, count, chunk):
    def body(i):
        _, au = apply_op(coefs, u, i, chunk)
        res[pl.ds(i - start, chunk)] = f_at(i) - au

    over(start, count, chunk, body)


def planes_at(ref, lead, chunk):
    if lead is None:
        return lambda i: ref[pl.ds(i, chunk)]
    return lambda i: ref[lead, pl.ds(i, chunk)]


def kernel(peers, dims, rhs, alpha, beta, out, sc):
    n_x, n_y = peers
    n = n_x * n_y
    g_x, g_y = lax.axis_index("gx"), lax.axis_index("gy")
    place = (g_x, g_y)
    me = g_x * n_y + g_y
    (x0, y0, z0), (x1, y1, z1), (x2, y2, z2), (x3, y3, z3) = dims
    X2, Y2, X3, Y3 = n_x * x2, n_y * y2, n_x * x3, n_y * y3
    sems = (sc["halo_send"], sc["halo_recv"])

    barrier = pltpu.get_barrier_semaphore()

    def greet(t, carry):
        j = lax.rem(me + t, n)
        pl.semaphore_signal(barrier, inc=1, device_id=(lax.div(j, n_y), lax.rem(j, n_y)),
                            device_id_type=MESH)
        return carry

    lax.fori_loop(1, n, greet, 0)

    def exchange(name, slot, x_len, y_len):
        return Exchange(sc[name], sc[name + "_n"], sc[name + "_p"], sems, slot, x_len, y_len,
                        place, peers)

    ex_in = exchange("in0", 0, x0, y0)
    ex_ab = exchange("ab1", 1, x1, y1)
    ex_f1 = exchange("f1", 2, x1, y1)
    ex_u0 = exchange("u0", 3, x0, y0)
    ex_u1 = exchange("u1", 4, x1, y1)
    ex_v1 = exchange("v1", 5, x1, y1)

    def gather_start(slot, src, dst_of, junk):
        send, recv = sc["all_send"].at[slot], sc["all_recv"].at[slot]

        def one(t, carry):
            j = lax.rem(me + t, n)
            pltpu.make_async_remote_copy(
                src_ref=src, dst_ref=dst_of(), send_sem=send, recv_sem=recv,
                device_id=(lax.div(j, n_y), lax.rem(j, n_y)), device_id_type=MESH).start()
            return carry

        lax.fori_loop(1, n, one, 0)
        pltpu.make_async_copy(src, dst_of(), recv).start()
        pltpu.make_async_copy(src, junk, send).start()

    def gather_wait(slot, whole):
        pltpu.make_async_copy(whole, whole, sc["all_recv"].at[slot]).wait()
        pltpu.make_async_copy(whole, whole, sc["all_send"].at[slot]).wait()

    def mine(ref):
        return ref.at[pl.ds(g_x * x2, x2), pl.ds(pl.multiple_of(g_y * y2, y2), y2)]

    in0 = sc["in0"]
    for k, ref in enumerate((rhs, alpha, beta)):
        in0[k, pl.ds(HALO, x0), pl.ds(0, y0)] = ref[...]
    pl.semaphore_wait(barrier, n - 1)
    ex_in.start()

    a1, b1 = restrict_sum(alpha[...], LANES), restrict_sum(beta[...], LANES)
    row = iota((8, LANES), 0)
    tile = jnp.where(row == 0, jnp.max(alpha[...]), 0.0)
    for k, value in ((1, jnp.max(beta[...])), (2, jnp.max(a1)), (3, jnp.max(b1))):
        tile = jnp.where(row == k, value, tile)
    sc["top"][...] = tile
    gather_start(0, sc["top"], lambda: sc["tops"].at[me], sc["top_junk"])
    ab1 = sc["ab1"]
    ab1[0, pl.ds(HALO, x1), pl.ds(0, y1)] = a1
    ab1[1, pl.ds(HALO, x1), pl.ds(0, y1)] = b1
    ex_ab.start()
    sc["ab2_src"][...] = restrict_sum(a1, LANES) + roll(restrict_sum(b1, LANES), z2, 2)
    gather_start(1, sc["ab2_src"], lambda: mine(sc["ab2"]), sc["ab2_junk"])

    for ex in (ex_in, ex_ab, ex_f1, ex_u0, ex_u1, ex_v1):
        ex.clear()

    ex_in.finish()
    k0 = [sc[k] for k in ("dia0", "cx0", "cy0", "cz0")]
    lo = HALO
    build(0, 1, x0 + 4, 1, planes_at(in0, 1, 1), planes_at(in0, 2, 1), z0, True, k0)
    sc["cx0"][0:1] = jnp.where(jnp.minimum(in0[2, 0:1], in0[2, 1:2]) > 0.0,
                               0.5 * (in0[2, 0:1] + in0[2, 1:2]), 0.0)
    gather_wait(0, sc["tops"])
    tops = jnp.max(sc["tops"][...], axis=0)
    wide = jnp.concatenate([tops, tops], axis=1)
    upper0 = HELM_SHIFT * wide[0:1] + 12.0 * wide[1:2]
    upper1 = HELM_SHIFT * tops[2:3] + 12.0 * tops[3:4] / 4.0
    ch0 = cheb(upper0, PRE_STEPS)
    ch1 = cheb(upper1, PRE_STEPS)
    f0 = planes_at(in0, 0, 1)
    ua, ub, d0 = sc["ua0"], sc["ub0"], sc["d0"]
    first(ua, d0, f0, ch0[0][1], 0, x0 + 6, 1)
    sweep(k0, ua, ub, d0, f0, *ch0[1], 1, x0 + 4, 1)
    sweep(k0, ub, ua, d0, f0, *ch0[2], 2, x0 + 2, 1)
    sc["u0"][0, pl.ds(lo, x0), pl.ds(0, y0)] = ua[pl.ds(lo, x0), pl.ds(0, y0)]
    residual(k0, ua, f0, sc["r0"], lo, x0, 1)
    sc["f1"][0, pl.ds(HALO, x1), pl.ds(0, y1)] = restrict_sum(sc["r0"][:, 0:y0], LANES)
    ex_f1.start()
    ex_u0.start()

    ex_ab.finish()
    k1 = [sc[k] for k in ("dia1", "cx1", "cy1", "cz1")]
    build(1, 1, x1 + 4, 2, planes_at(ab1, 0, 2), planes_at(ab1, 1, 2), z1, True, k1)
    sc["cx1"][0:1] = jnp.where(jnp.minimum(ab1[1, 0:1], ab1[1, 1:2]) > 0.0,
                               0.125 * (ab1[1, 0:1] + ab1[1, 1:2]), 0.0)
    ex_f1.finish()
    f1 = planes_at(sc["f1"], 0, 2)
    ua1, ub1, d1 = sc["ua1"], sc["ub1"], sc["d1"]
    first(ua1, d1, f1, ch1[0][1], 0, x1 + 6, 2)
    sweep(k1, ua1, ub1, d1, f1, *ch1[1], 1, x1 + 4, 2)
    sweep(k1, ub1, ua1, d1, f1, *ch1[2], 2, x1 + 2, 2)
    residual(k1, ua1, f1, sc["r1"], HALO, x1, 2)
    sc["f2_src"][...] = restrict_sum(sc["r1"][:, 0:y1], LANES)
    gather_start(2, sc["f2_src"], lambda: mine(sc["f2"]), sc["f2_junk"])
    sc["u1"][0, pl.ds(HALO, x1), pl.ds(0, y1)] = ua1[pl.ds(HALO, x1), pl.ds(0, y1)]
    ex_u1.start()

    k2 = [sc[k] for k in ("dia2", "cx2", "cy2", "cz2")]
    k3 = [sc[k] for k in ("dia3", "cx3", "cy3", "cz3")]
    ua2, ub2, d2 = sc["ua2"], sc["ub2"], sc["d2"]
    ua3, ub3, d3, f3 = sc["ua3"], sc["ub3"], sc["d3"], sc["f3"]
    for ref, size in ((ua2, X2), (ub2, X2), (sc["cx2"], X2), (d2, X2),
                      (ua3, X3), (ub3, X3), (sc["cx3"], X3), (d3, X3)):
        for at in (0, size + 1):
            ref[at] = jnp.zeros(ref.shape[1:], jnp.float32)
    gather_wait(1, sc["ab2"])
    q2 = 2 if X2 % 2 == 0 else 1
    q3 = X3 if X3 * Y3 <= 256 else 1
    fine = max(1, 256 // Y2) * 2
    fine = min(fine, X2)

    def unpack(i):
        both = sc["ab2"][pl.ds(i, q2)]
        lane = iota(both.shape, 2)
        ub2[pl.ds(i + 1, q2)] = jnp.where(lane < z2, both, 0.0)
        d2[pl.ds(i + 1, q2)] = jnp.where(lane < z2, roll(both, z2, 2), 0.0)

    over(0, X2, q2, unpack)

    def shrink(i):
        at, to = i * fine, i * (fine // 2)
        ub3[pl.ds(to + 1, fine // 2)] = restrict_sum(ub2[pl.ds(at + 1, fine)], LANES)
        d3[pl.ds(to + 1, fine // 2)] = restrict_sum(d2[pl.ds(at + 1, fine)], LANES)

    over(0, X2 // fine, 1, shrink)
    build(2, 1, X2, q2, planes_at(ub2, None, q2), planes_at(d2, None, q2), z2, False, k2)
    build(3, 1, X3, q3, planes_at(ub3, None, q3), planes_at(d3, None, q3), z3, False, k3)

    def largest(ref):
        best = jnp.max(jnp.max(ref[...], axis=0), axis=0, keepdims=True)
        return jnp.max(best, axis=1, keepdims=True) + jnp.zeros((1, LANES), jnp.float32)

    ch2 = cheb(HELM_SHIFT * largest(ub2) + 12.0 * largest(d2) / 16.0, PRE_STEPS)
    ch3 = cheb(HELM_SHIFT * largest(ub3) + 12.0 * largest(d3) / 64.0, COARSE_STEPS)
    gather_wait(2, sc["f2"])
    f2 = lambda i: sc["f2"][pl.ds(i - 1, q2)]
    first(ua2, d2, f2, ch2[0][1], 1, X2, q2)
    sweep(k2, ua2, ub2, d2, f2, *ch2[1], 1, X2, q2)
    sweep(k2, ub2, ua2, d2, f2, *ch2[2], 1, X2, q2)
    residual(k2, ua2, f2, ub2, 1, X2, q2)

    def shrink_f(i):
        at, to = i * fine, i * (fine // 2)
        f3[pl.ds(to + 1, fine // 2)] = restrict_sum(ub2[pl.ds(at, fine)], LANES)

    over(0, X2 // fine, 1, shrink_f)
    f3_at = planes_at(f3, None, q3)
    first(ua3, d3, f3_at, ch3[0][1], 1, X3, q3)
    now, later = ua3, ub3
    for a, b in ch3[1:]:
        sweep(k3, now, later, d3, f3_at, a, b, 1, X3, q3)
        now, later = later, now
    widen = pick(LANES, LANES, lambda i, j: (j >> 1) == i)
    part = max(1, fine // 2)
    rows3 = part * Y3

    def grow(i):
        small = dot(now[pl.ds(i * part + 1, part)].reshape(rows3, LANES), widen)
        tall = dot(pick(2 * rows3, rows3, lambda r, c: (r >> 1) == c), small)
        tall = tall.reshape(part, Y2, LANES)
        at = i * (2 * part) + 1
        lane = iota((Y2, LANES), 1)
        for k in range(part):
            add = jnp.where(lane < z2, tall[k], 0.0)
            ua2[at + 2 * k] = ua2[at + 2 * k] + add
            ua2[at + 2 * k + 1] = ua2[at + 2 * k + 1] + add

    over(0, X3 // part, 1, grow)
    ub2[0] = jnp.zeros(ub2.shape[1:], jnp.float32)
    ub2[X2 + 1] = jnp.zeros(ub2.shape[1:], jnp.float32)
    sweep(k2, ua2, ub2, d2, f2, None, ch2[0][1], 1, X2, q2)
    sweep(k2, ub2, ua2, d2, f2, *ch2[1], 1, X2, q2)
    sweep(k2, ua2, ub2, d2, f2, *ch2[2], 1, X2, q2)

    ex_u1.finish()
    here = pl.multiple_of(g_y * y2, 8)
    before = pl.multiple_of(jnp.maximum(g_y * y2 - 8, 0), 8)
    after = pl.multiple_of(jnp.minimum(g_y * y2 + y2, Y2 - 8), 8)
    turn = pick(y1 + 8, y2 + 16,
                lambda r, c: c == jnp.where(r < y1 + 4, 8 + (r >> 1), 6 + ((r - y1 - 4) >> 1)))
    u1 = sc["u1"]
    for k in range(x2 + 4):
        at = jnp.clip(g_x * x2 - 2 + k, 0, X2 - 1) + 1
        block = jnp.concatenate([ub2[at, pl.ds(before, 8)], ub2[at, pl.ds(here, y2)],
                                 ub2[at, pl.ds(after, 8)]], axis=0)
        block = dot(turn, dot(block, widen))
        for to in (2 * k - 1, 2 * k):
            if 0 <= to < x1 + 6:
                ua1[to] = u1[0, to] + block
    sweep(k1, ua1, ub1, d1, f1, None, ch1[0][1], 1, x1 + 4, 2)
    sweep(k1, ub1, ua1, d1, f1, *ch1[1], 2, x1 + 2, 2)
    sweep(k1, ua1, ub1, d1, f1, *ch1[2], 3, x1, 2)
    sc["v1"][0, pl.ds(HALO, x1), pl.ds(0, y1)] = ub1[pl.ds(HALO, x1), pl.ds(0, y1)]
    ex_v1.start()

    ex_u0.finish()
    ex_v1.finish()
    v1, u0 = sc["v1"], sc["u0"]
    widen0 = pick(z1, z0, lambda i, j: (j >> 1) == i)
    turn0 = pick(y0 + 8, y1 + 8,
                 lambda r, c: c == jnp.where(r < y0 + 4, r >> 1, y1 + 6 + ((r - y0 - 4) >> 1)))
    for k in range(x1 + 4):
        block = dot(dot(turn0, v1[0, k + 1]), widen0)
        for to in (2 * k - 1, 2 * k):
            if 0 <= to < x0 + 6:
                ua[to] = u0[0, to] + block
    sweep(k0, ua, ub, d0, f0, None, ch0[0][1], 1, x0 + 4, 1)
    sweep(k0, ub, ua, d0, f0, *ch0[1], 2, x0 + 2, 1)

    def last(i):
        mid, au = apply_op(k0, ua, i, 1)
        a, b = ch0[2]
        value = mid + (a * d0[pl.ds(i, 1)] + b * (f0(i) - au))
        out[pl.ds(i - lo, 1)] = value[:, 0:y0]

    over(lo, x0, 1, last)


def local(peers, rhs_field, alpha_coef, beta_coef):
    n_x, n_y = peers
    n = n_x * n_y
    x0, y0, z0 = rhs_field.shape
    dims = [(x0 >> k, y0 >> k, z0 >> k) for k in range(4)]
    (x0, y0, z0), (x1, y1, z1), (x2, y2, z2), (x3, y3, z3) = dims
    X2, Y2, X3, Y3 = n_x * x2, n_y * y2, n_x * x3, n_y * y3
    wide = {"in0": (3, x0, y0, z0), "ab1": (2, x1, y1, z1), "f1": (1, x1, y1, z1),
            "u0": (1, x0, y0, z0), "u1": (1, x1, y1, z1), "v1": (1, x1, y1, z1)}
    shapes = {}
    for name, (k, x, y, z) in wide.items():
        shapes[name] = (k, x + 2 * HALO, y + 8, z)
        shapes[name + "_n"] = shapes[name + "_p"] = (k, x + 2 * HALO, 8, z)
    full0, full1 = (x0 + 6, y0 + 8, z0), (x1 + 6, y1 + 8, z1)
    full2, full3 = (X2 + 2, Y2, LANES), (X3 + 2, Y3, LANES)
    for name, full in (("0", full0), ("1", full1), ("2", full2), ("3", full3)):
        for stem in ("dia", "cx", "cy", "cz", "ua", "ub", "d"):
            shapes[stem + name] = full
    shapes["f3"] = full3
    shapes["r0"], shapes["r1"] = (x0, y0 + 8, z0), (x1, y1 + 8, z1)
    shapes["ab2"] = shapes["f2"] = (X2, Y2, LANES)
    for stem in ("ab2", "f2"):
        shapes[stem + "_src"] = shapes[stem + "_junk"] = (x2, y2, LANES)
    shapes["top"] = shapes["top_junk"] = (8, LANES)
    shapes["tops"] = (n, 8, LANES)
    scratch = {name: pltpu.VMEM(shape, jnp.float32) for name, shape in shapes.items()}
    scratch["halo_send"] = pltpu.SemaphoreType.DMA((6, 8))
    scratch["halo_recv"] = pltpu.SemaphoreType.DMA((6, 8))
    scratch["all_send"] = pltpu.SemaphoreType.DMA((3,))
    scratch["all_recv"] = pltpu.SemaphoreType.DMA((3,))
    return pl.pallas_call(
        functools.partial(kernel, peers, dims),
        out_shape=jax.ShapeDtypeStruct(rhs_field.shape, jnp.float32),
        in_specs=[pl.BlockSpec(memory_space=pltpu.VMEM)] * 3,
        out_specs=pl.BlockSpec(memory_space=pltpu.VMEM),
        scratch_shapes=[scratch],
        compiler_params=pltpu.CompilerParams(
            collective_id=0, has_side_effects=True, vmem_limit_bytes=62 * 2**20),
    )(rhs_field, alpha_coef, beta_coef)


def solution(mesh):
    peers = (mesh.shape["gx"], mesh.shape["gy"])
    spec = P("gx", "gy", None)
    return jax.shard_map(functools.partial(local, peers), mesh=mesh, in_specs=(spec,) * 3,
                         out_specs=spec, check_vma=False)
```

```python
import functools

import jax
import jax.numpy as jnp
from jax import lax
from jax.experimental import pallas as pl
from jax.experimental.pallas import tpu as pltpu
from jax.sharding import PartitionSpec as P

PRE_STEPS = 3
POST_STEPS = 3
COARSE_STEPS = 8
HELM_SHIFT = 0.05
LOW_FRACTION = 0.1
LANES = 128
HALO = 3
MESH = pl.DeviceIdType.MESH
DIRS = [(1, 0), (-1, 0), (0, 1), (0, -1), (1, 1), (1, -1), (-1, 1), (-1, -1)]
HIGH = lax.Precision.HIGHEST


def dot(a, b):
    return jnp.dot(a, b, precision=HIGH, preferred_element_type=jnp.float32)


def iota(shape, dim):
    return lax.broadcasted_iota(jnp.int32, shape, dim)


def pick(rows, cols, cond):
    return cond(iota((rows, cols), 0), iota((rows, cols), 1)).astype(jnp.float32)


def roll(x, shift, axis):
    return pltpu.roll(x, shift % x.shape[axis], axis)


def restrict_sum(values, out_lanes):
    planes, rows, lanes = values.shape
    pairs = values.reshape(planes // 2, 2, rows, lanes)
    summed = (pairs[:, 0] + pairs[:, 1]).reshape(planes // 2 * rows, lanes)
    narrow = dot(summed, pick(lanes, out_lanes, lambda i, j: (i >> 1) == j))
    total = planes // 2 * rows
    small = dot(pick(total // 2, total, lambda i, j: (j >> 1) == i), narrow)
    return (0.125 * small).reshape(planes // 2, rows // 2, out_lanes)


class Exchange:
    def __init__(self, buf, sems, slot, x_len, y_len, place, peers):
        self.buf = buf
        self.send, self.recv = sems
        self.slot, self.x_len, self.y_len = slot, x_len, y_len
        self.place, self.peers = place, peers

    def region(self, dx, dy):
        x_len, y_len = self.x_len, self.y_len
        if dx == 0:
            src_x = dst_x = pl.ds(HALO, x_len)
        elif dx == 1:
            src_x, dst_x = pl.ds(x_len, HALO), pl.ds(0, HALO)
        else:
            src_x, dst_x = pl.ds(HALO, HALO), pl.ds(x_len + HALO, HALO)
        if dy == 0:
            return (self.buf.at[:, src_x, pl.ds(0, y_len)],
                    self.buf.at[:, dst_x, pl.ds(0, y_len)])
        src_y, dst_y = (y_len - 4, y_len + 4) if dy == 1 else (0, y_len)
        return self.buf.at[:, src_x, pl.ds(src_y, 4)], self.buf.at[:, dst_x, pl.ds(dst_y, 4)]

    def inside(self, dx, dy):
        x, y = self.place[0] + dx, self.place[1] + dy
        return (x >= 0) & (x < self.peers[0]) & (y >= 0) & (y < self.peers[1])

    def copy(self, k):
        dx, dy = DIRS[k]
        src, dst = self.region(dx, dy)
        return pltpu.make_async_remote_copy(
            src_ref=src, dst_ref=dst,
            send_sem=self.send.at[self.slot, k], recv_sem=self.recv.at[self.slot, k],
            device_id=(self.place[0] + dx, self.place[1] + dy), device_id_type=MESH)

    def clear(self):
        for dx, dy in DIRS:
            @pl.when(jnp.logical_not(self.inside(-dx, -dy)))
            def _():
                _, dst = self.region(dx, dy)
                dst[...] = jnp.zeros(dst.shape, jnp.float32)

    def start(self):
        for k, (dx, dy) in enumerate(DIRS):
            @pl.when(self.inside(dx, dy))
            def _():
                self.copy(k).start()

    def finish(self):
        for k, (dx, dy) in enumerate(DIRS):
            @pl.when(self.inside(dx, dy))
            def _():
                self.copy(k).wait_send()

            @pl.when(self.inside(-dx, -dy))
            def _():
                self.copy(k).wait_recv()


def over(start, count, chunk, body):
    if count == chunk:
        body(start)
        return

    times = count // chunk
    group = max(k for k in range(1, 6) if times % k == 0)

    def step(i, carry):
        for k in range(group):
            body(start + (i * group + k) * chunk)
        return carry

    if times == group:
        step(0, 0)
    else:
        lax.fori_loop(0, times // group, step, 0)


def build(level, start, count, chunk, alpha_at, beta_at, z_len, wrap_y, coefs):
    dia, c_x, c_y, c_z = coefs
    h = 0.5 / 4.0**level

    def body(i):
        b = beta_at(i)
        up, down = beta_at(i + 1), beta_at(i - 1)
        shape = b.shape
        lane, row = iota(shape, 2), iota(shape, 1)
        y_up, y_down = roll(b, -1, 1), roll(b, 1, 1)
        if not wrap_y:
            y_up = jnp.where(row == shape[1] - 1, 0.0, y_up)
            y_down = jnp.where(row == 0, 0.0, y_down)
        z_up = jnp.where(lane == z_len - 1, 0.0, roll(b, -1, 2))
        z_down = jnp.where(lane == 0, 0.0, roll(b, 1, 2))
        total = 6.0 * b + (up + down) + (y_up + y_down) + (z_up + z_down)
        dia[pl.ds(i, chunk)] = HELM_SHIFT * alpha_at(i) + h * total
        for out, near in ((c_x, up), (c_y, y_up), (c_z, z_up)):
            out[pl.ds(i, chunk)] = jnp.where(jnp.minimum(b, near) > 0.0, h * (b + near), 0.0)

    over(start, count, chunk, body)


def apply_op(coefs, u, i, chunk):
    dia, c_x, c_y, c_z = coefs
    here = pl.ds(i, chunk)
    mid = u[here]
    y_c, z_c = c_y[here], c_z[here]
    off = c_x[here] * u[pl.ds(i + 1, chunk)] + c_x[pl.ds(i - 1, chunk)] * u[pl.ds(i - 1, chunk)]
    off += y_c * roll(mid, -1, 1) + roll(y_c * mid, 1, 1)
    off += z_c * roll(mid, -1, 2) + roll(z_c * mid, 1, 2)
    return mid, dia[here] * mid - off


def cheb(upper, steps):
    lower = LOW_FRACTION * upper
    middle, half = 0.5 * (upper + lower), 0.5 * (upper - lower)
    scaled = middle / half
    factor = 1.0 / scaled
    out = [(None, 1.0 / middle)]
    for _ in range(1, steps):
        new = 1.0 / (2.0 * scaled - factor)
        out.append((new * factor, 2.0 * new / half))
        factor = new
    return out


def sweep(coefs, u, u_new, d, f_at, a, b, start, count, chunk):
    def body(i):
        mid, au = apply_op(coefs, u, i, chunk)
        step = b * (f_at(i) - au)
        if a is not None:
            step += a * d[pl.ds(i, chunk)]
        d[pl.ds(i, chunk)] = step
        u_new[pl.ds(i, chunk)] = mid + step

    over(start, count, chunk, body)


def first(u, d, f_at, b, start, count, chunk):
    def body(i):
        step = b * f_at(i)
        d[pl.ds(i, chunk)] = step
        u[pl.ds(i, chunk)] = step

    over(start, count, chunk, body)


def residual(coefs, u, f_at, res, start, count, chunk):
    def body(i):
        _, au = apply_op(coefs, u, i, chunk)
        res[pl.ds(i - start, chunk)] = f_at(i) - au

    over(start, count, chunk, body)


def planes_at(ref, lead, chunk):
    if lead is None:
        return lambda i: ref[pl.ds(i, chunk)]
    return lambda i: ref[lead, pl.ds(i, chunk)]


def kernel(peers, dims, rhs, alpha, beta, out, sc):
    n_x, n_y = peers
    n = n_x * n_y
    g_x, g_y = lax.axis_index("gx"), lax.axis_index("gy")
    place = (g_x, g_y)
    me = g_x * n_y + g_y
    (x0, y0, z0), (x1, y1, z1), (x2, y2, z2), (x3, y3, z3) = dims
    X2, Y2, X3, Y3 = n_x * x2, n_y * y2, n_x * x3, n_y * y3
    sems = (sc["halo_send"], sc["halo_recv"])

    barrier = pltpu.get_barrier_semaphore()

    def greet(t, carry):
        j = lax.rem(me + t, n)
        pl.semaphore_signal(barrier, inc=1, device_id=(lax.div(j, n_y), lax.rem(j, n_y)),
                            device_id_type=MESH)
        return carry

    lax.fori_loop(1, n, greet, 0)

    def exchange(name, slot, x_len, y_len):
        return Exchange(sc[name], sems, slot, x_len, y_len,
                        place, peers)

    ex_in = exchange("in0", 0, x0, y0)
    ex_ab = exchange("ab1", 1, x1, y1)
    ex_f1 = exchange("f1", 2, x1, y1)
    ex_u0 = exchange("u0", 3, x0, y0)
    ex_u1 = exchange("u1", 4, x1, y1)
    ex_v1 = exchange("v1", 5, x1, y1)

    def gather_start(slot, src, dst_of, junk):
        send, recv = sc["all_send"].at[slot], sc["all_recv"].at[slot]

        def one(t, carry):
            j = lax.rem(me + t, n)
            pltpu.make_async_remote_copy(
                src_ref=src, dst_ref=dst_of(), send_sem=send, recv_sem=recv,
                device_id=(lax.div(j, n_y), lax.rem(j, n_y)), device_id_type=MESH).start()
            return carry

        lax.fori_loop(1, n, one, 0)
        pltpu.make_async_copy(src, dst_of(), recv).start()
        pltpu.make_async_copy(src, junk, send).start()

    def gather_wait(slot, whole):
        pltpu.make_async_copy(whole, whole, sc["all_recv"].at[slot]).wait()
        pltpu.make_async_copy(whole, whole, sc["all_send"].at[slot]).wait()

    def mine(ref, planes):
        return ref.at[pl.ds(g_x * planes, planes), pl.ds(pl.multiple_of(g_y * y2, y2), y2)]

    in0 = sc["in0"]
    for k, ref in enumerate((rhs, alpha, beta)):
        in0[k, pl.ds(HALO, x0), pl.ds(0, y0)] = ref[...]
    pl.semaphore_wait(barrier, n - 1)
    ex_in.start()

    a1, b1 = restrict_sum(alpha[...], LANES), restrict_sum(beta[...], LANES)
    kind = iota((1, LANES), 1) >> 5
    tile = jnp.full((1, LANES), jnp.max(alpha[...]))
    for k, value in ((1, jnp.max(beta[...])), (2, jnp.max(a1)), (3, jnp.max(b1))):
        tile = jnp.where(kind == k, value, tile)
    sc["top"][...] = tile
    gather_start(0, sc["top"], lambda: sc["tops"].at[me], sc["top_junk"])
    ab1 = sc["ab1"]
    ab1[0, pl.ds(HALO, x1), pl.ds(0, y1)] = a1
    ab1[1, pl.ds(HALO, x1), pl.ds(0, y1)] = b1
    ex_ab.start()
    sc["ab2_src"][...] = restrict_sum(a1, LANES) + roll(restrict_sum(b1, LANES), z2, 2)
    gather_start(1, sc["ab2_src"], lambda: mine(sc["ab2"], x2), sc["ab2_junk"])

    for ex in (ex_in, ex_ab, ex_f1, ex_u0, ex_u1, ex_v1):
        ex.clear()

    ex_in.finish()
    k0 = [sc[k] for k in ("dia0", "cx0", "cy0", "cz0")]
    lo = HALO
    build(0, 1, x0 + 4, 1, planes_at(in0, 1, 1), planes_at(in0, 2, 1), z0, True, k0)
    sc["cx0"][0:1] = jnp.where(jnp.minimum(in0[2, 0:1], in0[2, 1:2]) > 0.0,
                               0.5 * (in0[2, 0:1] + in0[2, 1:2]), 0.0)
    gather_wait(0, sc["tops"])
    tops = jnp.max(sc["tops"][...], axis=0)
    greatest = [jnp.max(jnp.where(kind == k, tops, 0.0), axis=1, keepdims=True) for k in range(4)]
    upper0 = HELM_SHIFT * greatest[0] + 12.0 * greatest[1] + jnp.zeros((1, z0), jnp.float32)
    upper1 = HELM_SHIFT * greatest[2] + 12.0 * greatest[3] / 4.0 + jnp.zeros((1, z1), jnp.float32)
    ch0 = cheb(upper0, PRE_STEPS)
    ch1 = cheb(upper1, PRE_STEPS)
    f0 = planes_at(in0, 0, 1)
    ua, ub, d0 = sc["ua0"], sc["ub0"], sc["d0"]
    first(ua, d0, f0, ch0[0][1], 0, x0 + 6, 1)
    sweep(k0, ua, ub, d0, f0, *ch0[1], 1, x0 + 4, 1)
    sweep(k0, ub, ua, d0, f0, *ch0[2], 2, x0 + 2, 1)
    sc["u0"][0, pl.ds(lo, x0), pl.ds(0, y0)] = ua[pl.ds(lo, x0), pl.ds(0, y0)]
    residual(k0, ua, f0, sc["r0"], lo, x0, 1)
    sc["f1"][0, pl.ds(HALO, x1), pl.ds(0, y1)] = restrict_sum(sc["r0"][:, 0:y0], LANES)
    ex_f1.start()
    ex_u0.start()

    ex_ab.finish()
    k1 = [sc[k] for k in ("dia1", "cx1", "cy1", "cz1")]
    build(1, 1, x1 + 4, 2, planes_at(ab1, 0, 2), planes_at(ab1, 1, 2), z1, True, k1)
    sc["cx1"][0:1] = jnp.where(jnp.minimum(ab1[1, 0:1], ab1[1, 1:2]) > 0.0,
                               0.125 * (ab1[1, 0:1] + ab1[1, 1:2]), 0.0)
    ex_f1.finish()
    f1 = planes_at(sc["f1"], 0, 2)
    ua1, ub1, d1 = sc["ua1"], sc["ub1"], sc["d1"]
    first(ua1, d1, f1, ch1[0][1], 0, x1 + 6, 2)
    sweep(k1, ua1, ub1, d1, f1, *ch1[1], 1, x1 + 4, 2)
    sweep(k1, ub1, ua1, d1, f1, *ch1[2], 2, x1 + 2, 2)
    residual(k1, ua1, f1, sc["r1"], HALO, x1, 2)
    f2_own = restrict_sum(sc["r1"][:, 0:y1], LANES).reshape(x2 // 2, 2, y2, LANES)
    sc["f2_src"][...] = f2_own[:, 0] + roll(f2_own[:, 1], z2, 2)
    gather_start(2, sc["f2_src"], lambda: mine(sc["f2_pair"], x2 // 2), sc["f2_junk"])
    sc["u1"][0, pl.ds(HALO, x1), pl.ds(0, y1)] = ua1[pl.ds(HALO, x1), pl.ds(0, y1)]
    ex_u1.start()

    k2 = [sc[k] for k in ("dia2", "cx2", "cy2", "cz2")]
    k3 = [sc[k] for k in ("dia3", "cx3", "cy3", "cz3")]
    ua2, ub2, d2 = sc["ua2"], sc["ub2"], sc["d2"]
    ua3, ub3, d3, f3 = sc["ua3"], sc["ub3"], sc["d3"], sc["f3"]
    for ref, size in ((ua2, X2), (ub2, X2), (sc["cx2"], X2), (d2, X2),
                      (ua3, X3), (ub3, X3), (sc["cx3"], X3), (d3, X3)):
        for at in (0, size + 1):
            ref[at] = jnp.zeros(ref.shape[1:], jnp.float32)
    gather_wait(1, sc["ab2"])
    q2 = 2 if X2 % 2 == 0 else 1
    q3 = X3 if X3 * Y3 <= 256 else 1
    fine = max(1, 256 // Y2) * 2
    fine = min(fine, X2)

    def unpack(i):
        both = sc["ab2"][pl.ds(i, q2)]
        lane = iota(both.shape, 2)
        ub2[pl.ds(i + 1, q2)] = jnp.where(lane < z2, both, 0.0)
        d2[pl.ds(i + 1, q2)] = jnp.where(lane < z2, roll(both, z2, 2), 0.0)

    over(0, X2, q2, unpack)

    def shrink(i):
        at, to = i * fine, i * (fine // 2)
        ub3[pl.ds(to + 1, fine // 2)] = restrict_sum(ub2[pl.ds(at + 1, fine)], LANES)
        d3[pl.ds(to + 1, fine // 2)] = restrict_sum(d2[pl.ds(at + 1, fine)], LANES)

    over(0, X2 // fine, 1, shrink)
    build(2, 1, X2, q2, planes_at(ub2, None, q2), planes_at(d2, None, q2), z2, False, k2)
    build(3, 1, X3, q3, planes_at(ub3, None, q3), planes_at(d3, None, q3), z3, False, k3)

    def largest(ref):
        best = jnp.max(jnp.max(ref[...], axis=0), axis=0, keepdims=True)
        return jnp.max(best, axis=1, keepdims=True) + jnp.zeros((1, LANES), jnp.float32)

    ch2 = cheb(HELM_SHIFT * largest(ub2) + 12.0 * largest(d2) / 16.0, PRE_STEPS)
    ch3 = cheb(HELM_SHIFT * largest(ub3) + 12.0 * largest(d3) / 64.0, COARSE_STEPS)
    gather_wait(2, sc["f2_pair"])

    def unpack_f(i):
        both = sc["f2_pair"][pl.ds(i, 1)]
        low = iota(both.shape, 2) < z2
        sc["f2"][pl.ds(2 * i, 1)] = jnp.where(low, both, 0.0)
        sc["f2"][pl.ds(2 * i + 1, 1)] = jnp.where(low, roll(both, z2, 2), 0.0)

    over(0, X2 // 2, 1, unpack_f)
    f2 = lambda i: sc["f2"][pl.ds(i - 1, q2)]
    first(ua2, d2, f2, ch2[0][1], 1, X2, q2)
    sweep(k2, ua2, ub2, d2, f2, *ch2[1], 1, X2, q2)
    sweep(k2, ub2, ua2, d2, f2, *ch2[2], 1, X2, q2)
    residual(k2, ua2, f2, ub2, 1, X2, q2)

    def shrink_f(i):
        at, to = i * fine, i * (fine // 2)
        f3[pl.ds(to + 1, fine // 2)] = restrict_sum(ub2[pl.ds(at, fine)], LANES)

    over(0, X2 // fine, 1, shrink_f)
    f3_at = planes_at(f3, None, q3)
    first(ua3, d3, f3_at, ch3[0][1], 1, X3, q3)
    now, later = ua3, ub3
    for a, b in ch3[1:]:
        sweep(k3, now, later, d3, f3_at, a, b, 1, X3, q3)
        now, later = later, now
    widen = pick(LANES, LANES, lambda i, j: (j >> 1) == i)
    part = max(1, fine // 2)
    rows3 = part * Y3

    def grow(i):
        small = dot(now[pl.ds(i * part + 1, part)].reshape(rows3, LANES), widen)
        tall = dot(pick(2 * rows3, rows3, lambda r, c: (r >> 1) == c), small)
        tall = tall.reshape(part, Y2, LANES)
        at = i * (2 * part) + 1
        lane = iota((Y2, LANES), 1)
        for k in range(part):
            add = jnp.where(lane < z2, tall[k], 0.0)
            ua2[at + 2 * k] = ua2[at + 2 * k] + add
            ua2[at + 2 * k + 1] = ua2[at + 2 * k + 1] + add

    over(0, X3 // part, 1, grow)
    ub2[0] = jnp.zeros(ub2.shape[1:], jnp.float32)
    ub2[X2 + 1] = jnp.zeros(ub2.shape[1:], jnp.float32)
    sweep(k2, ua2, ub2, d2, f2, None, ch2[0][1], 1, X2, q2)
    sweep(k2, ub2, ua2, d2, f2, *ch2[1], 1, X2, q2)
    sweep(k2, ua2, ub2, d2, f2, *ch2[2], 1, X2, q2)

    ex_u1.finish()
    here = pl.multiple_of(g_y * y2, 8)
    before = pl.multiple_of(jnp.maximum(g_y * y2 - 8, 0), 8)
    after = pl.multiple_of(jnp.minimum(g_y * y2 + y2, Y2 - 8), 8)
    turn = pick(y1 + 8, y2 + 16,
                lambda r, c: c == jnp.where(r < y1 + 4, 8 + (r >> 1), 6 + ((r - y1 - 4) >> 1)))
    u1 = sc["u1"]
    for k in range(x2 + 4):
        at = jnp.clip(g_x * x2 - 2 + k, 0, X2 - 1) + 1
        block = jnp.concatenate([ub2[at, pl.ds(before, 8)], ub2[at, pl.ds(here, y2)],
                                 ub2[at, pl.ds(after, 8)]], axis=0)
        block = dot(turn, dot(block, widen))
        for to in (2 * k - 1, 2 * k):
            if 0 <= to < x1 + 6:
                ua1[to] = u1[0, to] + block
    sweep(k1, ua1, ub1, d1, f1, None, ch1[0][1], 1, x1 + 4, 2)
    sweep(k1, ub1, ua1, d1, f1, *ch1[1], 2, x1 + 2, 2)
    sweep(k1, ua1, ub1, d1, f1, *ch1[2], 3, x1, 2)
    sc["v1"][0, pl.ds(HALO, x1), pl.ds(0, y1)] = ub1[pl.ds(HALO, x1), pl.ds(0, y1)]
    ex_v1.start()

    ex_u0.finish()
    ex_v1.finish()
    v1, u0 = sc["v1"], sc["u0"]
    widen0 = pick(z1, z0, lambda i, j: (j >> 1) == i)
    turn0 = pick(y0 + 8, y1 + 8,
                 lambda r, c: c == jnp.where(r < y0 + 4, r >> 1, y1 + 6 + ((r - y0 - 4) >> 1)))
    for k in range(x1 + 4):
        block = dot(dot(turn0, v1[0, k + 1]), widen0)
        for to in (2 * k - 1, 2 * k):
            if 0 <= to < x0 + 6:
                ua[to] = u0[0, to] + block
    sweep(k0, ua, ub, d0, f0, None, ch0[0][1], 1, x0 + 4, 1)
    sweep(k0, ub, ua, d0, f0, *ch0[1], 2, x0 + 2, 1)

    def last(i):
        mid, au = apply_op(k0, ua, i, 1)
        a, b = ch0[2]
        value = mid + (a * d0[pl.ds(i, 1)] + b * (f0(i) - au))
        out[pl.ds(i - lo, 1)] = value[:, 0:y0]

    over(lo, x0, 1, last)


def local(peers, rhs_field, alpha_coef, beta_coef):
    n_x, n_y = peers
    n = n_x * n_y
    x0, y0, z0 = rhs_field.shape
    dims = [(x0 >> k, y0 >> k, z0 >> k) for k in range(4)]
    (x0, y0, z0), (x1, y1, z1), (x2, y2, z2), (x3, y3, z3) = dims
    X2, Y2, X3, Y3 = n_x * x2, n_y * y2, n_x * x3, n_y * y3
    wide = {"in0": (3, x0, y0, z0), "ab1": (2, x1, y1, z1), "f1": (1, x1, y1, z1),
            "u0": (1, x0, y0, z0), "u1": (1, x1, y1, z1), "v1": (1, x1, y1, z1)}
    shapes = {}
    for name, (k, x, y, z) in wide.items():
        shapes[name] = (k, x + 2 * HALO, y + 8, z)
    full0, full1 = (x0 + 6, y0 + 8, z0), (x1 + 6, y1 + 8, z1)
    full2, full3 = (X2 + 2, Y2, LANES), (X3 + 2, Y3, LANES)
    for name, full in (("0", full0), ("1", full1), ("2", full2), ("3", full3)):
        for stem in ("dia", "cx", "cy", "cz", "ua", "ub", "d"):
            shapes[stem + name] = full
    shapes["f3"] = full3
    shapes["r0"], shapes["r1"] = (x0, y0 + 8, z0), (x1, y1 + 8, z1)
    shapes["ab2"] = shapes["f2"] = (X2, Y2, LANES)
    shapes["f2_pair"] = (X2 // 2, Y2, LANES)
    shapes["ab2_src"] = shapes["ab2_junk"] = (x2, y2, LANES)
    shapes["f2_src"] = shapes["f2_junk"] = (x2 // 2, y2, LANES)
    shapes["top"] = shapes["top_junk"] = (1, LANES)
    shapes["tops"] = (n, 1, LANES)
    scratch = {name: pltpu.VMEM(shape, jnp.float32) for name, shape in shapes.items()}
    scratch["halo_send"] = pltpu.SemaphoreType.DMA((6, 8))
    scratch["halo_recv"] = pltpu.SemaphoreType.DMA((6, 8))
    scratch["all_send"] = pltpu.SemaphoreType.DMA((3,))
    scratch["all_recv"] = pltpu.SemaphoreType.DMA((3,))
    return pl.pallas_call(
        functools.partial(kernel, peers, dims),
        out_shape=jax.ShapeDtypeStruct(rhs_field.shape, jnp.float32),
        in_specs=[pl.BlockSpec(memory_space=pltpu.VMEM)] * 3,
        out_specs=pl.BlockSpec(memory_space=pltpu.VMEM),
        scratch_shapes=[scratch],
        compiler_params=pltpu.CompilerParams(
            collective_id=0, has_side_effects=True, vmem_limit_bytes=62 * 2**20),
    )(rhs_field, alpha_coef, beta_coef)


def solution(mesh):
    peers = (mesh.shape["gx"], mesh.shape["gy"])
    spec = P("gx", "gy", None)
    return jax.shard_map(functools.partial(local, peers), mesh=mesh, in_specs=(spec,) * 3,
                         out_specs=spec, check_vma=False)
```

```python
import functools

import jax
import jax.numpy as jnp
from jax import lax
from jax.experimental import pallas as pl
from jax.experimental.pallas import tpu as pltpu
from jax.sharding import PartitionSpec as P

PRE_STEPS = 3
POST_STEPS = 3
COARSE_STEPS = 8
HELM_SHIFT = 0.05
LOW_FRACTION = 0.1
LANES = 128
HALO = 3
MESH = pl.DeviceIdType.MESH
DIRS = [(1, 0), (-1, 0), (0, 1), (0, -1), (1, 1), (1, -1), (-1, 1), (-1, -1)]
HIGH = lax.Precision.HIGHEST


def dot(a, b):
    return jnp.dot(a, b, precision=HIGH, preferred_element_type=jnp.float32)


def iota(shape, dim):
    return lax.broadcasted_iota(jnp.int32, shape, dim)


def pick(rows, cols, cond):
    return cond(iota((rows, cols), 0), iota((rows, cols), 1)).astype(jnp.float32)


def roll(x, shift, axis):
    return pltpu.roll(x, shift % x.shape[axis], axis)


def restrict_sum(values, out_lanes):
    planes, rows, lanes = values.shape
    pairs = values.reshape(planes // 2, 2, rows, lanes)
    summed = (pairs[:, 0] + pairs[:, 1]).reshape(planes // 2 * rows, lanes)
    narrow = dot(summed, pick(lanes, out_lanes, lambda i, j: (i >> 1) == j))
    total = planes // 2 * rows
    small = dot(pick(total // 2, total, lambda i, j: (j >> 1) == i), narrow)
    return (0.125 * small).reshape(planes // 2, rows // 2, out_lanes)


class Exchange:
    def __init__(self, buf, sems, slot, x_len, y_len, place, peers):
        self.buf = buf
        self.send, self.recv = sems
        self.slot, self.x_len, self.y_len = slot, x_len, y_len
        self.place, self.peers = place, peers

    def region(self, dx, dy):
        x_len, y_len = self.x_len, self.y_len
        if dx == 0:
            src_x = dst_x = pl.ds(HALO, x_len)
        elif dx == 1:
            src_x, dst_x = pl.ds(x_len, HALO), pl.ds(0, HALO)
        else:
            src_x, dst_x = pl.ds(HALO, HALO), pl.ds(x_len + HALO, HALO)
        if dy == 0:
            return (self.buf.at[:, src_x, pl.ds(0, y_len)],
                    self.buf.at[:, dst_x, pl.ds(0, y_len)])
        src_y, dst_y = (y_len - 4, y_len + 4) if dy == 1 else (0, y_len)
        return self.buf.at[:, src_x, pl.ds(src_y, 4)], self.buf.at[:, dst_x, pl.ds(dst_y, 4)]

    def inside(self, dx, dy):
        x, y = self.place[0] + dx, self.place[1] + dy
        return (x >= 0) & (x < self.peers[0]) & (y >= 0) & (y < self.peers[1])

    def copy(self, k):
        dx, dy = DIRS[k]
        src, dst = self.region(dx, dy)
        return pltpu.make_async_remote_copy(
            src_ref=src, dst_ref=dst,
            send_sem=self.send.at[self.slot, k], recv_sem=self.recv.at[self.slot, k],
            device_id=(self.place[0] + dx, self.place[1] + dy), device_id_type=MESH)

    def clear(self):
        for dx, dy in DIRS:
            @pl.when(jnp.logical_not(self.inside(-dx, -dy)))
            def _():
                _, dst = self.region(dx, dy)
                dst[...] = jnp.zeros(dst.shape, jnp.float32)

    def start(self):
        for k, (dx, dy) in enumerate(DIRS):
            @pl.when(self.inside(dx, dy))
            def _():
                self.copy(k).start()

    def finish(self):
        for k, (dx, dy) in enumerate(DIRS):
            @pl.when(self.inside(dx, dy))
            def _():
                self.copy(k).wait_send()

            @pl.when(self.inside(-dx, -dy))
            def _():
                self.copy(k).wait_recv()


def over(start, count, chunk, body):
    if count == chunk:
        body(start)
        return

    times = count // chunk
    group = max(k for k in range(1, 6) if times % k == 0)

    def step(i, carry):
        for k in range(group):
            body(start + (i * group + k) * chunk)
        return carry

    if times == group:
        step(0, 0)
    else:
        lax.fori_loop(0, times // group, step, 0)


def build(level, start, count, chunk, alpha_at, beta_at, z_len, wrap_y, coefs):
    dia, c_x, c_y, c_z = coefs
    h = 0.5 / 4.0**level

    def body(i):
        b = beta_at(i)
        up, down = beta_at(i + 1), beta_at(i - 1)
        shape = b.shape
        lane, row = iota(shape, 2), iota(shape, 1)
        y_up, y_down = roll(b, -1, 1), roll(b, 1, 1)
        if not wrap_y:
            y_up = jnp.where(row == shape[1] - 1, 0.0, y_up)
            y_down = jnp.where(row == 0, 0.0, y_down)
        z_up = jnp.where(lane == z_len - 1, 0.0, roll(b, -1, 2))
        z_down = jnp.where(lane == 0, 0.0, roll(b, 1, 2))
        total = 6.0 * b + (up + down) + (y_up + y_down) + (z_up + z_down)
        dia[pl.ds(i, chunk)] = HELM_SHIFT * alpha_at(i) + h * total
        for out, near in ((c_x, up), (c_y, y_up), (c_z, z_up)):
            out[pl.ds(i, chunk)] = jnp.where(jnp.minimum(b, near) > 0.0, h * (b + near), 0.0)

    over(start, count, chunk, body)


def apply_op(coefs, u, i, chunk):
    dia, c_x, c_y, c_z = coefs
    here = pl.ds(i, chunk)
    mid = u[here]
    y_c, z_c = c_y[here], c_z[here]
    off = c_x[here] * u[pl.ds(i + 1, chunk)] + c_x[pl.ds(i - 1, chunk)] * u[pl.ds(i - 1, chunk)]
    off += y_c * roll(mid, -1, 1) + roll(y_c * mid, 1, 1)
    off += z_c * roll(mid, -1, 2) + roll(z_c * mid, 1, 2)
    return mid, dia[here] * mid - off


def cheb(upper, steps):
    middle, half = 0.5 * (1.0 + LOW_FRACTION), 0.5 * (1.0 - LOW_FRACTION)
    scaled = middle / half
    factor = 1.0 / scaled
    inverse = 1.0 / upper
    out = [(None, inverse * (1.0 / middle))]
    for _ in range(1, steps):
        new = 1.0 / (2.0 * scaled - factor)
        out.append((new * factor, inverse * (2.0 * new / half)))
        factor = new
    return out


def sweep(coefs, u, u_new, d, f_at, a, b, start, count, chunk):
    def body(i):
        mid, au = apply_op(coefs, u, i, chunk)
        step = b * (f_at(i) - au)
        if a is not None:
            step += a * d[pl.ds(i, chunk)]
        d[pl.ds(i, chunk)] = step
        u_new[pl.ds(i, chunk)] = mid + step

    over(start, count, chunk, body)


def first(u, d, f_at, b, start, count, chunk):
    def body(i):
        step = b * f_at(i)
        d[pl.ds(i, chunk)] = step
        u[pl.ds(i, chunk)] = step

    over(start, count, chunk, body)


def residual(coefs, u, f_at, res, start, count, chunk):
    def body(i):
        _, au = apply_op(coefs, u, i, chunk)
        res[pl.ds(i - start, chunk)] = f_at(i) - au

    over(start, count, chunk, body)


def planes_at(ref, lead, chunk):
    if lead is None:
        return lambda i: ref[pl.ds(i, chunk)]
    return lambda i: ref[lead, pl.ds(i, chunk)]


def kernel(peers, dims, rhs, alpha, beta, out, sc):
    n_x, n_y = peers
    g_x, g_y = lax.axis_index("gx"), lax.axis_index("gy")
    place = (g_x, g_y)
    (x0, y0, z0), (x1, y1, z1), (x2, y2, z2), (x3, y3, z3) = dims
    X2, Y2, X3, Y3 = n_x * x2, n_y * y2, n_x * x3, n_y * y3
    sems = (sc["halo_send"], sc["halo_recv"])

    barrier = pltpu.get_barrier_semaphore()

    def each(count, body):
        if count <= 8:
            for t in range(1, count):
                body(t)
        else:
            def step(t, carry):
                body(t)
                return carry

            lax.fori_loop(1, count, step, 0)

    along_x = lambda t: (lax.rem(g_x + t, n_x), g_y)
    along_y = lambda t: (g_x, lax.rem(g_y + t, n_y))

    def greet(device):
        pl.semaphore_signal(barrier, inc=1, device_id=device, device_id_type=MESH)

    each(n_x, lambda t: greet(along_x(t)))
    each(n_y, lambda t: greet(along_y(t)))
    corners = 0
    for dx, dy in DIRS[4:]:
        x, y = g_x + dx, g_y + dy
        there = (x >= 0) & (x < n_x) & (y >= 0) & (y < n_y)
        corners = corners + there.astype(jnp.int32)

        @pl.when(there)
        def _():
            greet((x, y))

    in0 = sc["in0"]
    loads = [pltpu.make_async_copy(ref, in0.at[k, pl.ds(HALO, x0), pl.ds(0, y0)], sc["load"].at[k])
             for k, ref in enumerate((rhs, alpha, beta))]
    for load in loads:
        load.start()

    def exchange(name, slot, x_len, y_len):
        return Exchange(sc[name], sems, slot, x_len, y_len,
                        place, peers)

    ex_in = exchange("in0", 0, x0, y0)
    ex_ab = exchange("ab1", 1, x1, y1)
    ex_f1 = exchange("f1", 2, x1, y1)
    ex_u0 = exchange("u0", 3, x0, y0)
    ex_u1 = exchange("u1", 4, x1, y1)
    ex_v1 = exchange("v1", 5, x1, y1)

    def spread(slot, src, dst, count, where):
        def one(t):
            pltpu.make_async_remote_copy(
                src_ref=src, dst_ref=dst, send_sem=sc["all_send"].at[slot],
                recv_sem=sc["all_recv"].at[slot], device_id=where(t), device_id_type=MESH).start()

        each(count, one)

    def spread_wait(slot, size):
        pltpu.make_async_copy(size, size, sc["all_recv"].at[slot]).wait()
        pltpu.make_async_copy(size, size, sc["all_send"].at[slot]).wait()

    def slab(ref, planes):
        return ref.at[pl.ds(g_x * planes, planes)]

    def gather_y(slot, ref, planes, value):
        own = ref.at[pl.ds(g_x * planes, planes), pl.ds(pl.multiple_of(g_y * y2, 8), y2)]
        own[...] = value
        spread(slot, own, own, n_y, along_y)

    def gather_x(slot, ref, planes):
        spread_wait(slot, ref.at[pl.ds(0, planes), pl.ds(0, (n_y - 1) * y2)])
        spread(slot + 1, slab(ref, planes), slab(ref, planes), n_x, along_x)

    def gather_wait(slot, ref, planes):
        spread_wait(slot + 1, ref.at[pl.ds(0, (n_x - 1) * planes)])

    for ex in (ex_in, ex_ab, ex_f1, ex_u0, ex_u1, ex_v1):
        ex.clear()
    for load in loads:
        load.wait()
    pl.semaphore_wait(barrier, n_x - 1 + n_y - 1 + corners)
    ex_in.start()

    a0 = in0[1, pl.ds(HALO, x0), pl.ds(0, y0)]
    b0 = in0[2, pl.ds(HALO, x0), pl.ds(0, y0)]
    a1, b1 = restrict_sum(a0, LANES), restrict_sum(b0, LANES)
    kind = iota((1, LANES), 1) >> 5
    tile = jnp.full((1, LANES), jnp.max(a0))
    for k, value in ((1, jnp.max(b0)), (2, jnp.max(a1)), (3, jnp.max(b1))):
        tile = jnp.where(kind == k, value, tile)
    top_y, top_x = sc["top_y"], sc["top_x"]
    top_y[g_y] = tile
    spread(0, top_y.at[g_y], top_y.at[g_y], n_y, along_y)
    ab1 = sc["ab1"]
    ab1[0, pl.ds(HALO, x1), pl.ds(0, y1)] = a1
    ab1[1, pl.ds(HALO, x1), pl.ds(0, y1)] = b1
    ex_ab.start()
    both2 = restrict_sum(a1, LANES) + roll(restrict_sum(b1, LANES), z2, 2)
    gather_y(2, sc["ab2"], x2, both2)
    spread_wait(0, top_y.at[pl.ds(0, n_y - 1)])
    top_x[g_x] = jnp.max(top_y[...], axis=0)
    spread(1, top_x.at[g_x], top_x.at[g_x], n_x, along_x)

    ex_in.finish()
    k0 = [sc[k] for k in ("dia0", "cx0", "cy0", "cz0")]
    lo = HALO
    build(0, 1, x0 + 4, 1, planes_at(in0, 1, 1), planes_at(in0, 2, 1), z0, True, k0)
    sc["cx0"][0:1] = jnp.where(jnp.minimum(in0[2, 0:1], in0[2, 1:2]) > 0.0,
                               0.5 * (in0[2, 0:1] + in0[2, 1:2]), 0.0)
    gather_x(2, sc["ab2"], x2)
    spread_wait(1, top_x.at[pl.ds(0, n_x - 1)])
    tops = jnp.max(top_x[...], axis=0)
    greatest = [jnp.max(jnp.where(kind == k, tops, 0.0), axis=1, keepdims=True) for k in range(4)]
    upper0 = HELM_SHIFT * greatest[0] + 12.0 * greatest[1] + jnp.zeros((1, z0), jnp.float32)
    upper1 = HELM_SHIFT * greatest[2] + 12.0 * greatest[3] / 4.0 + jnp.zeros((1, z1), jnp.float32)
    ch0 = cheb(upper0, PRE_STEPS)
    ch1 = cheb(upper1, PRE_STEPS)
    f0 = planes_at(in0, 0, 1)
    ua, ub, d0 = sc["ua0"], sc["ub0"], sc["d0"]
    first(ua, d0, f0, ch0[0][1], 0, x0 + 6, 1)
    sweep(k0, ua, ub, d0, f0, *ch0[1], 1, x0 + 4, 1)
    sweep(k0, ub, ua, d0, f0, *ch0[2], 2, x0 + 2, 1)
    sc["u0"][0, pl.ds(lo, x0), pl.ds(0, y0)] = ua[pl.ds(lo, x0), pl.ds(0, y0)]
    residual(k0, ua, f0, sc["r0"], lo, x0, 1)
    sc["f1"][0, pl.ds(HALO, x1), pl.ds(0, y1)] = restrict_sum(sc["r0"][:, 0:y0], LANES)
    ex_f1.start()
    ex_u0.start()

    ex_ab.finish()
    k1 = [sc[k] for k in ("dia1", "cx1", "cy1", "cz1")]
    build(1, 1, x1 + 4, 2, planes_at(ab1, 0, 2), planes_at(ab1, 1, 2), z1, True, k1)
    sc["cx1"][0:1] = jnp.where(jnp.minimum(ab1[1, 0:1], ab1[1, 1:2]) > 0.0,
                               0.125 * (ab1[1, 0:1] + ab1[1, 1:2]), 0.0)
    ex_f1.finish()
    f1 = planes_at(sc["f1"], 0, 2)
    ua1, ub1, d1 = sc["ua1"], sc["ub1"], sc["d1"]
    first(ua1, d1, f1, ch1[0][1], 0, x1 + 6, 2)
    sweep(k1, ua1, ub1, d1, f1, *ch1[1], 1, x1 + 4, 2)
    sweep(k1, ub1, ua1, d1, f1, *ch1[2], 2, x1 + 2, 2)
    residual(k1, ua1, f1, sc["r1"], HALO, x1, 2)
    f2_own = restrict_sum(sc["r1"][:, 0:y1], LANES).reshape(x2 // 2, 2, y2, LANES)
    gather_y(4, sc["f2_pair"], x2 // 2, f2_own[:, 0] + roll(f2_own[:, 1], z2, 2))
    sc["u1"][0, pl.ds(HALO, x1), pl.ds(0, y1)] = ua1[pl.ds(HALO, x1), pl.ds(0, y1)]
    ex_u1.start()

    k2 = [sc[k] for k in ("dia2", "cx2", "cy2", "cz2")]
    k3 = [sc[k] for k in ("dia3", "cx3", "cy3", "cz3")]
    ua2, ub2, d2 = sc["ua2"], sc["ub2"], sc["d2"]
    ua3, ub3, d3, f3 = sc["ua3"], sc["ub3"], sc["d3"], sc["f3"]
    for ref, size in ((ua2, X2), (ub2, X2), (sc["cx2"], X2), (d2, X2),
                      (ua3, X3), (ub3, X3), (sc["cx3"], X3), (d3, X3)):
        for at in (0, size + 1):
            ref[at] = jnp.zeros(ref.shape[1:], jnp.float32)
    gather_wait(2, sc["ab2"], x2)
    gather_x(4, sc["f2_pair"], x2 // 2)
    q2 = 2 if X2 % 2 == 0 else 1
    q3 = X3 if X3 * Y3 <= 256 else 1
    fine = max(1, 256 // Y2) * 2
    fine = min(fine, X2)

    def unpack(i):
        both = sc["ab2"][pl.ds(i, q2)]
        lane = iota(both.shape, 2)
        ub2[pl.ds(i + 1, q2)] = jnp.where(lane < z2, both, 0.0)
        d2[pl.ds(i + 1, q2)] = jnp.where(lane < z2, roll(both, z2, 2), 0.0)

    over(0, X2, q2, unpack)

    def shrink(i):
        at, to = i * fine, i * (fine // 2)
        ub3[pl.ds(to + 1, fine // 2)] = restrict_sum(ub2[pl.ds(at + 1, fine)], LANES)
        d3[pl.ds(to + 1, fine // 2)] = restrict_sum(d2[pl.ds(at + 1, fine)], LANES)

    over(0, X2 // fine, 1, shrink)
    build(2, 1, X2, q2, planes_at(ub2, None, q2), planes_at(d2, None, q2), z2, False, k2)
    build(3, 1, X3, q3, planes_at(ub3, None, q3), planes_at(d3, None, q3), z3, False, k3)

    def largest(ref):
        best = jnp.max(jnp.max(ref[...], axis=0), axis=0, keepdims=True)
        return jnp.max(best, axis=1, keepdims=True) + jnp.zeros((1, LANES), jnp.float32)

    ch2 = cheb(HELM_SHIFT * largest(ub2) + 12.0 * largest(d2) / 16.0, PRE_STEPS)
    ch3 = cheb(HELM_SHIFT * largest(ub3) + 12.0 * largest(d3) / 64.0, COARSE_STEPS)
    gather_wait(4, sc["f2_pair"], x2 // 2)

    def unpack_f(i):
        both = sc["f2_pair"][pl.ds(i, 1)]
        low = iota(both.shape, 2) < z2
        sc["f2"][pl.ds(2 * i, 1)] = jnp.where(low, both, 0.0)
        sc["f2"][pl.ds(2 * i + 1, 1)] = jnp.where(low, roll(both, z2, 2), 0.0)

    over(0, X2 // 2, 1, unpack_f)
    f2 = lambda i: sc["f2"][pl.ds(i - 1, q2)]
    first(ua2, d2, f2, ch2[0][1], 1, X2, q2)
    sweep(k2, ua2, ub2, d2, f2, *ch2[1], 1, X2, q2)
    sweep(k2, ub2, ua2, d2, f2, *ch2[2], 1, X2, q2)
    residual(k2, ua2, f2, ub2, 1, X2, q2)

    def shrink_f(i):
        at, to = i * fine, i * (fine // 2)
        f3[pl.ds(to + 1, fine // 2)] = restrict_sum(ub2[pl.ds(at, fine)], LANES)

    over(0, X2 // fine, 1, shrink_f)
    f3_at = planes_at(f3, None, q3)
    first(ua3, d3, f3_at, ch3[0][1], 1, X3, q3)
    now, later = ua3, ub3
    for a, b in ch3[1:]:
        sweep(k3, now, later, d3, f3_at, a, b, 1, X3, q3)
        now, later = later, now
    widen = pick(LANES, LANES, lambda i, j: (j >> 1) == i)
    part = max(1, fine // 2)
    rows3 = part * Y3

    def grow(i):
        small = dot(now[pl.ds(i * part + 1, part)].reshape(rows3, LANES), widen)
        tall = dot(pick(2 * rows3, rows3, lambda r, c: (r >> 1) == c), small)
        tall = tall.reshape(part, Y2, LANES)
        at = i * (2 * part) + 1
        lane = iota((Y2, LANES), 1)
        for k in range(part):
            add = jnp.where(lane < z2, tall[k], 0.0)
            ua2[at + 2 * k] = ua2[at + 2 * k] + add
            ua2[at + 2 * k + 1] = ua2[at + 2 * k + 1] + add

    over(0, X3 // part, 1, grow)
    ub2[0] = jnp.zeros(ub2.shape[1:], jnp.float32)
    ub2[X2 + 1] = jnp.zeros(ub2.shape[1:], jnp.float32)
    sweep(k2, ua2, ub2, d2, f2, None, ch2[0][1], 1, X2, q2)
    sweep(k2, ub2, ua2, d2, f2, *ch2[1], 1, X2, q2)
    sweep(k2, ua2, ub2, d2, f2, *ch2[2], 1, X2, q2)

    ex_u1.finish()
    here = pl.multiple_of(g_y * y2, 8)
    before = pl.multiple_of(jnp.maximum(g_y * y2 - 8, 0), 8)
    after = pl.multiple_of(jnp.minimum(g_y * y2 + y2, Y2 - 8), 8)
    turn = pick(y1 + 8, y2 + 16,
                lambda r, c: c == jnp.where(r < y1 + 4, 8 + (r >> 1), 6 + ((r - y1 - 4) >> 1)))
    u1 = sc["u1"]
    for k in range(x2 + 4):
        at = jnp.clip(g_x * x2 - 2 + k, 0, X2 - 1) + 1
        block = jnp.concatenate([ub2[at, pl.ds(before, 8)], ub2[at, pl.ds(here, y2)],
                                 ub2[at, pl.ds(after, 8)]], axis=0)
        block = dot(turn, dot(block, widen))
        for to in (2 * k - 1, 2 * k):
            if 0 <= to < x1 + 6:
                ua1[to] = u1[0, to] + block
    sweep(k1, ua1, ub1, d1, f1, None, ch1[0][1], 1, x1 + 4, 2)
    sweep(k1, ub1, ua1, d1, f1, *ch1[1], 2, x1 + 2, 2)
    sweep(k1, ua1, ub1, d1, f1, *ch1[2], 3, x1, 2)
    sc["v1"][0, pl.ds(HALO, x1), pl.ds(0, y1)] = ub1[pl.ds(HALO, x1), pl.ds(0, y1)]
    ex_v1.start()

    ex_u0.finish()
    ex_v1.finish()
    v1, u0 = sc["v1"], sc["u0"]
    widen0 = pick(z1, z0, lambda i, j: (j >> 1) == i)
    turn0 = pick(y0 + 8, y1 + 8,
                 lambda r, c: c == jnp.where(r < y0 + 4, r >> 1, y1 + 6 + ((r - y0 - 4) >> 1)))
    for k in range(x1 + 4):
        block = dot(dot(turn0, v1[0, k + 1]), widen0)
        for to in (2 * k - 1, 2 * k):
            if 0 <= to < x0 + 6:
                ua[to] = u0[0, to] + block
    sweep(k0, ua, ub, d0, f0, None, ch0[0][1], 1, x0 + 4, 1)
    sweep(k0, ub, ua, d0, f0, *ch0[1], 2, x0 + 2, 1)

    def last(i):
        mid, au = apply_op(k0, ua, i, 1)
        a, b = ch0[2]
        value = mid + (a * d0[pl.ds(i, 1)] + b * (f0(i) - au))
        out[pl.ds(i - lo, 1)] = value[:, 0:y0]

    over(lo, x0, 1, last)


def local(peers, rhs_field, alpha_coef, beta_coef):
    n_x, n_y = peers
    x0, y0, z0 = rhs_field.shape
    dims = [(x0 >> k, y0 >> k, z0 >> k) for k in range(4)]
    (x0, y0, z0), (x1, y1, z1), (x2, y2, z2), (x3, y3, z3) = dims
    X2, Y2, X3, Y3 = n_x * x2, n_y * y2, n_x * x3, n_y * y3
    wide = {"in0": (3, x0, y0, z0), "ab1": (2, x1, y1, z1), "f1": (1, x1, y1, z1),
            "u0": (1, x0, y0, z0), "u1": (1, x1, y1, z1), "v1": (1, x1, y1, z1)}
    shapes = {}
    for name, (k, x, y, z) in wide.items():
        shapes[name] = (k, x + 2 * HALO, y + 8, z)
    full0, full1 = (x0 + 6, y0 + 8, z0), (x1 + 6, y1 + 8, z1)
    full2, full3 = (X2 + 2, Y2, LANES), (X3 + 2, Y3, LANES)
    for name, full in (("0", full0), ("1", full1), ("2", full2), ("3", full3)):
        for stem in ("dia", "cx", "cy", "cz", "ua", "ub", "d"):
            shapes[stem + name] = full
    shapes["f3"] = full3
    shapes["r0"], shapes["r1"] = (x0, y0 + 8, z0), (x1, y1 + 8, z1)
    shapes["ab2"] = shapes["f2"] = (X2, Y2, LANES)
    shapes["f2_pair"] = (X2 // 2, Y2, LANES)
    shapes["top_y"], shapes["top_x"] = (n_y, 1, LANES), (n_x, 1, LANES)
    scratch = {name: pltpu.VMEM(shape, jnp.float32) for name, shape in shapes.items()}
    scratch["halo_send"] = pltpu.SemaphoreType.DMA((6, 8))
    scratch["halo_recv"] = pltpu.SemaphoreType.DMA((6, 8))
    scratch["all_send"] = pltpu.SemaphoreType.DMA((6,))
    scratch["all_recv"] = pltpu.SemaphoreType.DMA((6,))
    scratch["load"] = pltpu.SemaphoreType.DMA((3,))
    return pl.pallas_call(
        functools.partial(kernel, peers, dims),
        out_shape=jax.ShapeDtypeStruct(rhs_field.shape, jnp.float32),
        in_specs=[pl.BlockSpec(memory_space=pl.ANY)] * 3,
        out_specs=pl.BlockSpec(memory_space=pltpu.VMEM),
        scratch_shapes=[scratch],
        compiler_params=pltpu.CompilerParams(
            collective_id=0, has_side_effects=True, vmem_limit_bytes=62 * 2**20),
    )(rhs_field, alpha_coef, beta_coef)


def solution(mesh):
    peers = (mesh.shape["gx"], mesh.shape["gy"])
    spec = P("gx", "gy", None)
    return jax.shard_map(functools.partial(local, peers), mesh=mesh, in_specs=(spec,) * 3,
                         out_specs=spec, check_vma=False)
```

```python
import functools

import jax
import jax.numpy as jnp
from jax import lax
from jax.experimental import pallas as pl
from jax.experimental.pallas import tpu as pltpu
from jax.sharding import PartitionSpec as P

PRE_STEPS = 3
POST_STEPS = 3
COARSE_STEPS = 8
HELM_SHIFT = 0.05
LOW_FRACTION = 0.1
LANES = 128
HALO = 3
MESH = pl.DeviceIdType.MESH
DIRS = [(1, 0), (-1, 0), (0, 1), (0, -1), (1, 1), (1, -1), (-1, 1), (-1, -1)]


def dot(a, b):
    total, rest = None, b if a.dtype == jnp.bfloat16 else a
    for _ in range(3):
        part = rest.astype(jnp.bfloat16)
        rest = rest - part.astype(jnp.float32)
        pair = (a, part) if a.dtype == jnp.bfloat16 else (part, b)
        term = jnp.dot(*pair, preferred_element_type=jnp.float32)
        total = term if total is None else total + term
    return total


def iota(shape, dim):
    return lax.broadcasted_iota(jnp.int32, shape, dim)


def pick(rows, cols, cond):
    return cond(iota((rows, cols), 0), iota((rows, cols), 1)).astype(jnp.float32).astype(jnp.bfloat16)


def roll(x, shift, axis):
    return pltpu.roll(x, shift % x.shape[axis], axis)


def restrict_sum(values, out_lanes):
    planes, rows, lanes = values.shape
    pairs = values.reshape(planes // 2, 2, rows, lanes)
    summed = (pairs[:, 0] + pairs[:, 1]).reshape(planes // 2 * rows, lanes)
    narrow = dot(summed, pick(lanes, out_lanes, lambda i, j: (i >> 1) == j))
    total = planes // 2 * rows
    small = dot(pick(total // 2, total, lambda i, j: (j >> 1) == i), narrow)
    return (0.125 * small).reshape(planes // 2, rows // 2, out_lanes)


class Exchange:
    def __init__(self, buf, sems, slot, x_len, y_len, place, peers):
        self.buf = buf
        self.send, self.recv = sems
        self.slot, self.x_len, self.y_len = slot, x_len, y_len
        self.place, self.peers = place, peers

    def region(self, dx, dy):
        x_len, y_len = self.x_len, self.y_len
        if dx == 0:
            src_x = dst_x = pl.ds(HALO, x_len)
        elif dx == 1:
            src_x, dst_x = pl.ds(x_len, HALO), pl.ds(0, HALO)
        else:
            src_x, dst_x = pl.ds(HALO, HALO), pl.ds(x_len + HALO, HALO)
        if dy == 0:
            return (self.buf.at[:, src_x, pl.ds(0, y_len)],
                    self.buf.at[:, dst_x, pl.ds(0, y_len)])
        src_y, dst_y = (y_len - 4, y_len + 4) if dy == 1 else (0, y_len)
        return self.buf.at[:, src_x, pl.ds(src_y, 4)], self.buf.at[:, dst_x, pl.ds(dst_y, 4)]

    def inside(self, dx, dy):
        x, y = self.place[0] + dx, self.place[1] + dy
        return (x >= 0) & (x < self.peers[0]) & (y >= 0) & (y < self.peers[1])

    def copy(self, k):
        dx, dy = DIRS[k]
        src, dst = self.region(dx, dy)
        return pltpu.make_async_remote_copy(
            src_ref=src, dst_ref=dst,
            send_sem=self.send.at[self.slot, k], recv_sem=self.recv.at[self.slot, k],
            device_id=(self.place[0] + dx, self.place[1] + dy), device_id_type=MESH)

    def clear(self):
        for dx, dy in DIRS:
            @pl.when(jnp.logical_not(self.inside(-dx, -dy)))
            def _():
                _, dst = self.region(dx, dy)
                dst[...] = jnp.zeros(dst.shape, jnp.float32)

    def start(self):
        for k, (dx, dy) in enumerate(DIRS):
            @pl.when(self.inside(dx, dy))
            def _():
                self.copy(k).start()

    def finish(self):
        for k, (dx, dy) in enumerate(DIRS):
            @pl.when(self.inside(dx, dy))
            def _():
                self.copy(k).wait_send()

            @pl.when(self.inside(-dx, -dy))
            def _():
                self.copy(k).wait_recv()


def over(start, count, chunk, body):
    if count == chunk:
        body(start)
        return

    times = count // chunk
    group = max(k for k in range(1, 6) if times % k == 0)

    def step(i, carry):
        for k in range(group):
            body(start + (i * group + k) * chunk)
        return carry

    if times == group:
        step(0, 0)
    else:
        lax.fori_loop(0, times // group, step, 0)


def build(level, start, count, chunk, alpha_at, beta_at, z_len, wrap_y, coefs):
    dia, c_x, c_y, c_z = coefs
    h = 0.5 / 4.0**level

    def body(i):
        b = beta_at(i)
        up, down = beta_at(i + 1), beta_at(i - 1)
        shape = b.shape
        lane, row = iota(shape, 2), iota(shape, 1)
        y_up, y_down = roll(b, -1, 1), roll(b, 1, 1)
        if not wrap_y:
            y_up = jnp.where(row == shape[1] - 1, 0.0, y_up)
            y_down = jnp.where(row == 0, 0.0, y_down)
        z_up = jnp.where(lane == z_len - 1, 0.0, roll(b, -1, 2))
        z_down = jnp.where(lane == 0, 0.0, roll(b, 1, 2))
        total = 6.0 * b + (up + down) + (y_up + y_down) + (z_up + z_down)
        dia[pl.ds(i, chunk)] = HELM_SHIFT * alpha_at(i) + h * total
        for out, near in ((c_x, up), (c_y, y_up), (c_z, z_up)):
            out[pl.ds(i, chunk)] = jnp.where(jnp.minimum(b, near) > 0.0, h * (b + near), 0.0)

    over(start, count, chunk, body)


def apply_op(coefs, u, i, chunk):
    dia, c_x, c_y, c_z = coefs
    here = pl.ds(i, chunk)
    mid = u[here]
    y_c, z_c = c_y[here], c_z[here]
    off = c_x[here] * u[pl.ds(i + 1, chunk)] + c_x[pl.ds(i - 1, chunk)] * u[pl.ds(i - 1, chunk)]
    off += y_c * roll(mid, -1, 1) + roll(y_c * mid, 1, 1)
    off += z_c * roll(mid, -1, 2) + roll(z_c * mid, 1, 2)
    return mid, dia[here] * mid - off


def cheb(upper, steps):
    middle, half = 0.5 * (1.0 + LOW_FRACTION), 0.5 * (1.0 - LOW_FRACTION)
    scaled = middle / half
    factor = 1.0 / scaled
    inverse = 1.0 / upper
    out = [(None, inverse * (1.0 / middle))]
    for _ in range(1, steps):
        new = 1.0 / (2.0 * scaled - factor)
        out.append((new * factor, inverse * (2.0 * new / half)))
        factor = new
    return out


def sweep(coefs, u, u_new, d, f_at, a, b, start, count, chunk):
    def body(i):
        mid, au = apply_op(coefs, u, i, chunk)
        step = b * (f_at(i) - au)
        if a is not None:
            step += a * d[pl.ds(i, chunk)]
        d[pl.ds(i, chunk)] = step
        u_new[pl.ds(i, chunk)] = mid + step

    over(start, count, chunk, body)


def first(u, d, f_at, b, start, count, chunk):
    def body(i):
        step = b * f_at(i)
        d[pl.ds(i, chunk)] = step
        u[pl.ds(i, chunk)] = step

    over(start, count, chunk, body)


def residual(coefs, u, f_at, res, start, count, chunk):
    def body(i):
        _, au = apply_op(coefs, u, i, chunk)
        res[pl.ds(i - start, chunk)] = f_at(i) - au

    over(start, count, chunk, body)


def planes_at(ref, lead, chunk):
    if lead is None:
        return lambda i: ref[pl.ds(i, chunk)]
    return lambda i: ref[lead, pl.ds(i, chunk)]


def kernel(peers, dims, rhs, alpha, beta, out, sc):
    n_x, n_y = peers
    g_x, g_y = lax.axis_index("gx"), lax.axis_index("gy")
    place = (g_x, g_y)
    (x0, y0, z0), (x1, y1, z1), (x2, y2, z2), (x3, y3, z3) = dims
    X2, Y2, X3, Y3 = n_x * x2, n_y * y2, n_x * x3, n_y * y3
    sems = (sc["halo_send"], sc["halo_recv"])

    barrier = pltpu.get_barrier_semaphore()

    def each(count, body):
        if count <= 8:
            for t in range(1, count):
                body(t)
        else:
            def step(t, carry):
                body(t)
                return carry

            lax.fori_loop(1, count, step, 0)

    along_x = lambda t: (lax.rem(g_x + t, n_x), g_y)
    along_y = lambda t: (g_x, lax.rem(g_y + t, n_y))

    def greet(device):
        pl.semaphore_signal(barrier, inc=1, device_id=device, device_id_type=MESH)

    each(n_x, lambda t: greet(along_x(t)))
    each(n_y, lambda t: greet(along_y(t)))
    corners = 0
    for dx, dy in DIRS[4:]:
        x, y = g_x + dx, g_y + dy
        there = (x >= 0) & (x < n_x) & (y >= 0) & (y < n_y)
        corners = corners + there.astype(jnp.int32)

        @pl.when(there)
        def _():
            greet((x, y))

    in0 = sc["in0"]
    loads = [pltpu.make_async_copy(ref, in0.at[k, pl.ds(HALO, x0), pl.ds(0, y0)], sc["load"].at[k])
             for k, ref in enumerate((rhs, alpha, beta))]
    for load in loads:
        load.start()

    def exchange(name, slot, x_len, y_len):
        return Exchange(sc[name], sems, slot, x_len, y_len,
                        place, peers)

    ex_in = exchange("in0", 0, x0, y0)
    ex_ab = exchange("ab1", 1, x1, y1)
    ex_f1 = exchange("f1", 2, x1, y1)
    ex_u0 = exchange("u0", 3, x0, y0)
    ex_u1 = exchange("u1", 4, x1, y1)
    ex_v1 = exchange("v1", 5, x1, y1)

    def spread(slot, src, dst, count, where):
        def one(t):
            pltpu.make_async_remote_copy(
                src_ref=src, dst_ref=dst, send_sem=sc["all_send"].at[slot],
                recv_sem=sc["all_recv"].at[slot], device_id=where(t), device_id_type=MESH).start()

        each(count, one)

    def spread_wait(slot, size):
        pltpu.make_async_copy(size, size, sc["all_recv"].at[slot]).wait()
        pltpu.make_async_copy(size, size, sc["all_send"].at[slot]).wait()

    def slab(ref, planes):
        return ref.at[pl.ds(g_x * planes, planes)]

    def gather_y(slot, ref, planes, value):
        own = ref.at[pl.ds(g_x * planes, planes), pl.ds(pl.multiple_of(g_y * y2, 8), y2)]
        own[...] = value
        spread(slot, own, own, n_y, along_y)

    def gather_x(slot, ref, planes):
        spread_wait(slot, ref.at[pl.ds(0, planes), pl.ds(0, (n_y - 1) * y2)])
        spread(slot + 1, slab(ref, planes), slab(ref, planes), n_x, along_x)

    def gather_wait(slot, ref, planes):
        spread_wait(slot + 1, ref.at[pl.ds(0, (n_x - 1) * planes)])

    for ex in (ex_in, ex_ab, ex_f1, ex_u0, ex_u1, ex_v1):
        ex.clear()
    for load in loads:
        load.wait()
    pl.semaphore_wait(barrier, n_x - 1 + n_y - 1 + corners)
    ex_in.start()

    a0 = in0[1, pl.ds(HALO, x0), pl.ds(0, y0)]
    b0 = in0[2, pl.ds(HALO, x0), pl.ds(0, y0)]
    a1, b1 = restrict_sum(a0, LANES), restrict_sum(b0, LANES)
    kind = iota((1, LANES), 1) >> 5
    tile = jnp.full((1, LANES), jnp.max(a0))
    for k, value in ((1, jnp.max(b0)), (2, jnp.max(a1)), (3, jnp.max(b1))):
        tile = jnp.where(kind == k, value, tile)
    top_y, top_x = sc["top_y"], sc["top_x"]
    top_y[g_y] = tile
    spread(0, top_y.at[g_y], top_y.at[g_y], n_y, along_y)
    ab1 = sc["ab1"]
    ab1[0, pl.ds(HALO, x1), pl.ds(0, y1)] = a1
    ab1[1, pl.ds(HALO, x1), pl.ds(0, y1)] = b1
    ex_ab.start()
    both2 = restrict_sum(a1, LANES) + roll(restrict_sum(b1, LANES), z2, 2)
    gather_y(2, sc["ab2"], x2, both2)
    spread_wait(0, top_y.at[pl.ds(0, n_y - 1)])
    top_x[g_x] = jnp.max(top_y[...], axis=0)
    spread(1, top_x.at[g_x], top_x.at[g_x], n_x, along_x)

    ex_in.finish()
    k0 = [sc[k] for k in ("dia0", "cx0", "cy0", "cz0")]
    lo = HALO
    build(0, 1, x0 + 4, 1, planes_at(in0, 1, 1), planes_at(in0, 2, 1), z0, True, k0)
    sc["cx0"][0:1] = jnp.where(jnp.minimum(in0[2, 0:1], in0[2, 1:2]) > 0.0,
                               0.5 * (in0[2, 0:1] + in0[2, 1:2]), 0.0)
    gather_x(2, sc["ab2"], x2)
    spread_wait(1, top_x.at[pl.ds(0, n_x - 1)])
    tops = jnp.max(top_x[...], axis=0)
    greatest = [jnp.max(jnp.where(kind == k, tops, 0.0), axis=1, keepdims=True) for k in range(4)]
    upper0 = HELM_SHIFT * greatest[0] + 12.0 * greatest[1] + jnp.zeros((1, z0), jnp.float32)
    upper1 = HELM_SHIFT * greatest[2] + 12.0 * greatest[3] / 4.0 + jnp.zeros((1, z1), jnp.float32)
    ch0 = cheb(upper0, PRE_STEPS)
    ch1 = cheb(upper1, PRE_STEPS)
    f0 = planes_at(in0, 0, 1)
    ua, ub, d0 = sc["ua0"], sc["ub0"], sc["d0"]
    first(ua, d0, f0, ch0[0][1], 0, x0 + 6, 1)
    sweep(k0, ua, ub, d0, f0, *ch0[1], 1, x0 + 4, 1)
    sweep(k0, ub, ua, d0, f0, *ch0[2], 2, x0 + 2, 1)
    sc["u0"][0, pl.ds(lo, x0), pl.ds(0, y0)] = ua[pl.ds(lo, x0), pl.ds(0, y0)]
    residual(k0, ua, f0, sc["r0"], lo, x0, 1)
    sc["f1"][0, pl.ds(HALO, x1), pl.ds(0, y1)] = restrict_sum(sc["r0"][:, 0:y0], LANES)
    ex_f1.start()
    ex_u0.start()

    ex_ab.finish()
    k1 = [sc[k] for k in ("dia1", "cx1", "cy1", "cz1")]
    build(1, 1, x1 + 4, 2, planes_at(ab1, 0, 2), planes_at(ab1, 1, 2), z1, True, k1)
    sc["cx1"][0:1] = jnp.where(jnp.minimum(ab1[1, 0:1], ab1[1, 1:2]) > 0.0,
                               0.125 * (ab1[1, 0:1] + ab1[1, 1:2]), 0.0)
    ex_f1.finish()
    f1 = planes_at(sc["f1"], 0, 2)
    ua1, ub1, d1 = sc["ua1"], sc["ub1"], sc["d1"]
    first(ua1, d1, f1, ch1[0][1], 0, x1 + 6, 2)
    sweep(k1, ua1, ub1, d1, f1, *ch1[1], 1, x1 + 4, 2)
    sweep(k1, ub1, ua1, d1, f1, *ch1[2], 2, x1 + 2, 2)
    residual(k1, ua1, f1, sc["r1"], HALO, x1, 2)
    f2_own = restrict_sum(sc["r1"][:, 0:y1], LANES).reshape(x2 // 2, 2, y2, LANES)
    gather_y(4, sc["f2_pair"], x2 // 2, f2_own[:, 0] + roll(f2_own[:, 1], z2, 2))
    sc["u1"][0, pl.ds(HALO, x1), pl.ds(0, y1)] = ua1[pl.ds(HALO, x1), pl.ds(0, y1)]
    ex_u1.start()

    k2 = [sc[k] for k in ("dia2", "cx2", "cy2", "cz2")]
    k3 = [sc[k] for k in ("dia3", "cx3", "cy3", "cz3")]
    ua2, ub2, d2 = sc["ua2"], sc["ub2"], sc["d2"]
    ua3, ub3, d3, f3 = sc["ua3"], sc["ub3"], sc["d3"], sc["f3"]
    for ref, size in ((ua2, X2), (ub2, X2), (sc["cx2"], X2), (d2, X2),
                      (ua3, X3), (ub3, X3), (sc["cx3"], X3), (d3, X3)):
        for at in (0, size + 1):
            ref[at] = jnp.zeros(ref.shape[1:], jnp.float32)
    gather_wait(2, sc["ab2"], x2)
    gather_x(4, sc["f2_pair"], x2 // 2)
    q2 = 2 if X2 % 2 == 0 else 1
    q3 = X3 if X3 * Y3 <= 256 else 1
    fine = max(1, 256 // Y2) * 2
    fine = min(fine, X2)

    def unpack(i):
        both = sc["ab2"][pl.ds(i, q2)]
        lane = iota(both.shape, 2)
        ub2[pl.ds(i + 1, q2)] = jnp.where(lane < z2, both, 0.0)
        d2[pl.ds(i + 1, q2)] = jnp.where(lane < z2, roll(both, z2, 2), 0.0)

    over(0, X2, q2, unpack)

    def shrink(i):
        at, to = i * fine, i * (fine // 2)
        ub3[pl.ds(to + 1, fine // 2)] = restrict_sum(ub2[pl.ds(at + 1, fine)], LANES)
        d3[pl.ds(to + 1, fine // 2)] = restrict_sum(d2[pl.ds(at + 1, fine)], LANES)

    over(0, X2 // fine, 1, shrink)
    build(2, 1, X2, q2, planes_at(ub2, None, q2), planes_at(d2, None, q2), z2, False, k2)
    build(3, 1, X3, q3, planes_at(ub3, None, q3), planes_at(d3, None, q3), z3, False, k3)

    def largest(ref):
        best = jnp.max(jnp.max(ref[...], axis=0), axis=0, keepdims=True)
        return jnp.max(best, axis=1, keepdims=True) + jnp.zeros((1, LANES), jnp.float32)

    ch2 = cheb(HELM_SHIFT * largest(ub2) + 12.0 * largest(d2) / 16.0, PRE_STEPS)
    ch3 = cheb(HELM_SHIFT * largest(ub3) + 12.0 * largest(d3) / 64.0, COARSE_STEPS)
    gather_wait(4, sc["f2_pair"], x2 // 2)

    def unpack_f(i):
        both = sc["f2_pair"][pl.ds(i, 1)]
        low = iota(both.shape, 2) < z2
        sc["f2"][pl.ds(2 * i, 1)] = jnp.where(low, both, 0.0)
        sc["f2"][pl.ds(2 * i + 1, 1)] = jnp.where(low, roll(both, z2, 2), 0.0)

    over(0, X2 // 2, 1, unpack_f)
    f2 = lambda i: sc["f2"][pl.ds(i - 1, q2)]
    first(ua2, d2, f2, ch2[0][1], 1, X2, q2)
    sweep(k2, ua2, ub2, d2, f2, *ch2[1], 1, X2, q2)
    sweep(k2, ub2, ua2, d2, f2, *ch2[2], 1, X2, q2)
    residual(k2, ua2, f2, ub2, 1, X2, q2)

    def shrink_f(i):
        at, to = i * fine, i * (fine // 2)
        f3[pl.ds(to + 1, fine // 2)] = restrict_sum(ub2[pl.ds(at, fine)], LANES)

    over(0, X2 // fine, 1, shrink_f)
    f3_at = planes_at(f3, None, q3)
    first(ua3, d3, f3_at, ch3[0][1], 1, X3, q3)
    now, later = ua3, ub3
    for a, b in ch3[1:]:
        sweep(k3, now, later, d3, f3_at, a, b, 1, X3, q3)
        now, later = later, now
    widen = pick(LANES, LANES, lambda i, j: (j >> 1) == i)
    part = max(1, fine // 2)
    rows3 = part * Y3

    def grow(i):
        small = dot(now[pl.ds(i * part + 1, part)].reshape(rows3, LANES), widen)
        tall = dot(pick(2 * rows3, rows3, lambda r, c: (r >> 1) == c), small)
        tall = tall.reshape(part, Y2, LANES)
        at = i * (2 * part) + 1
        lane = iota((Y2, LANES), 1)
        for k in range(part):
            add = jnp.where(lane < z2, tall[k], 0.0)
            ua2[at + 2 * k] = ua2[at + 2 * k] + add
            ua2[at + 2 * k + 1] = ua2[at + 2 * k + 1] + add

    over(0, X3 // part, 1, grow)
    ub2[0] = jnp.zeros(ub2.shape[1:], jnp.float32)
    ub2[X2 + 1] = jnp.zeros(ub2.shape[1:], jnp.float32)
    sweep(k2, ua2, ub2, d2, f2, None, ch2[0][1], 1, X2, q2)
    sweep(k2, ub2, ua2, d2, f2, *ch2[1], 1, X2, q2)
    sweep(k2, ua2, ub2, d2, f2, *ch2[2], 1, X2, q2)

    ex_u1.finish()
    here = pl.multiple_of(g_y * y2, 8)
    before = pl.multiple_of(jnp.maximum(g_y * y2 - 8, 0), 8)
    after = pl.multiple_of(jnp.minimum(g_y * y2 + y2, Y2 - 8), 8)
    turn = pick(y1 + 8, y2 + 16,
                lambda r, c: c == jnp.where(r < y1 + 4, 8 + (r >> 1), 6 + ((r - y1 - 4) >> 1)))
    u1 = sc["u1"]
    for k in range(x2 + 4):
        at = jnp.clip(g_x * x2 - 2 + k, 0, X2 - 1) + 1
        block = jnp.concatenate([ub2[at, pl.ds(before, 8)], ub2[at, pl.ds(here, y2)],
                                 ub2[at, pl.ds(after, 8)]], axis=0)
        block = dot(turn, dot(block, widen))
        for to in (2 * k - 1, 2 * k):
            if 0 <= to < x1 + 6:
                ua1[to] = u1[0, to] + block
    sweep(k1, ua1, ub1, d1, f1, None, ch1[0][1], 1, x1 + 4, 2)
    sweep(k1, ub1, ua1, d1, f1, *ch1[1], 2, x1 + 2, 2)
    sweep(k1, ua1, ub1, d1, f1, *ch1[2], 3, x1, 2)
    sc["v1"][0, pl.ds(HALO, x1), pl.ds(0, y1)] = ub1[pl.ds(HALO, x1), pl.ds(0, y1)]
    ex_v1.start()

    ex_u0.finish()
    ex_v1.finish()
    v1, u0 = sc["v1"], sc["u0"]
    widen0 = pick(z1, z0, lambda i, j: (j >> 1) == i)
    turn0 = pick(y0 + 8, y1 + 8,
                 lambda r, c: c == jnp.where(r < y0 + 4, r >> 1, y1 + 6 + ((r - y0 - 4) >> 1)))
    for k in range(x1 + 4):
        block = dot(dot(turn0, v1[0, k + 1]), widen0)
        for to in (2 * k - 1, 2 * k):
            if 0 <= to < x0 + 6:
                ua[to] = u0[0, to] + block
    sweep(k0, ua, ub, d0, f0, None, ch0[0][1], 1, x0 + 4, 1)
    sweep(k0, ub, ua, d0, f0, *ch0[1], 2, x0 + 2, 1)

    def last(i):
        mid, au = apply_op(k0, ua, i, 1)
        a, b = ch0[2]
        value = mid + (a * d0[pl.ds(i, 1)] + b * (f0(i) - au))
        out[pl.ds(i - lo, 1)] = value[:, 0:y0]

    over(lo, x0, 1, last)


def local(peers, rhs_field, alpha_coef, beta_coef):
    n_x, n_y = peers
    x0, y0, z0 = rhs_field.shape
    dims = [(x0 >> k, y0 >> k, z0 >> k) for k in range(4)]
    (x0, y0, z0), (x1, y1, z1), (x2, y2, z2), (x3, y3, z3) = dims
    X2, Y2, X3, Y3 = n_x * x2, n_y * y2, n_x * x3, n_y * y3
    wide = {"in0": (3, x0, y0, z0), "ab1": (2, x1, y1, z1), "f1": (1, x1, y1, z1),
            "u0": (1, x0, y0, z0), "u1": (1, x1, y1, z1), "v1": (1, x1, y1, z1)}
    shapes = {}
    for name, (k, x, y, z) in wide.items():
        shapes[name] = (k, x + 2 * HALO, y + 8, z)
    full0, full1 = (x0 + 6, y0 + 8, z0), (x1 + 6, y1 + 8, z1)
    full2, full3 = (X2 + 2, Y2, LANES), (X3 + 2, Y3, LANES)
    for name, full in (("0", full0), ("1", full1), ("2", full2), ("3", full3)):
        for stem in ("dia", "cx", "cy", "cz", "ua", "ub", "d"):
            shapes[stem + name] = full
    shapes["f3"] = full3
    shapes["r0"], shapes["r1"] = (x0, y0 + 8, z0), (x1, y1 + 8, z1)
    shapes["ab2"] = shapes["f2"] = (X2, Y2, LANES)
    shapes["f2_pair"] = (X2 // 2, Y2, LANES)
    shapes["top_y"], shapes["top_x"] = (n_y, 1, LANES), (n_x, 1, LANES)
    scratch = {name: pltpu.VMEM(shape, jnp.float32) for name, shape in shapes.items()}
    scratch["halo_send"] = pltpu.SemaphoreType.DMA((6, 8))
    scratch["halo_recv"] = pltpu.SemaphoreType.DMA((6, 8))
    scratch["all_send"] = pltpu.SemaphoreType.DMA((6,))
    scratch["all_recv"] = pltpu.SemaphoreType.DMA((6,))
    scratch["load"] = pltpu.SemaphoreType.DMA((3,))
    return pl.pallas_call(
        functools.partial(kernel, peers, dims),
        out_shape=jax.ShapeDtypeStruct(rhs_field.shape, jnp.float32),
        in_specs=[pl.BlockSpec(memory_space=pl.ANY)] * 3,
        out_specs=pl.BlockSpec(memory_space=pltpu.VMEM),
        scratch_shapes=[scratch],
        compiler_params=pltpu.CompilerParams(
            collective_id=0, has_side_effects=True, vmem_limit_bytes=62 * 2**20),
    )(rhs_field, alpha_coef, beta_coef)


def solution(mesh):
    peers = (mesh.shape["gx"], mesh.shape["gy"])
    spec = P("gx", "gy", None)
    return jax.shard_map(functools.partial(local, peers), mesh=mesh, in_specs=(spec,) * 3,
                         out_specs=spec, check_vma=False)
```
